32 devices in a mesh: gx: 2 (over y), gy: 4 (over z), gz: 4 (over x, core).
Axes of the slice: x: 2, y: 2, z: 4, core: 2. Of those that a mesh axis runs over, the one named last changes fastest.
Arguments:
- shape_coef: float32 [2, 4, 4, 4, 3, 169], P('gx', 'gy', 'gz')
- density_coef: float32 [2, 4, 4, 4, 3, 169], P('gx', 'gy', 'gz'), may hold values from -1.8 to 1.8
- pair_count: int32 [2, 4, 4], P('gx', 'gy', 'gz'), may hold values from 4 to 12, as said below
- pair_slots: int32 [2, 4, 4, 12, 2], P('gx', 'gy', 'gz'), may hold values from 0 to 107, as said below
Outputs:
- vel_coef: float32 [2, 4, 4, 4, 3, 169], P('gx', 'gy', 'gz')
The draws below stay inside these ranges and needn't reach their ends.
Inputs may be any that keep to these rules, and one draw needn't show every extreme that they name: `pair_count`: each device owns from 4 to 12 close pairs; some device owns exactly 12. `pair_slots`: an entry names a vesicle of the owner or of a device next to it (diagonals included) that exists in the grid; the first entry of every slot names a vesicle of the owner; the two vesicles of a slot differ; every vesicle is the first of one of its own device's first 4 slots; slots at or beyond the owner's pair_count are not read.
All inputs are finite; a program needn't handle non-finite values.
Results may differ from the reference program's by a relative error of at most 0.0003.
Values sent between devices are 32-bit elements; how exact they have to be, the bound alone decides.
A program may use at most 64 MiB of HBM per device.

```python
import math
import jax
import jax.numpy as jnp
import numpy as np
from jax import lax

P_SIZE = 12
Q = 24
V_DEV = 4
NC = 169
PAIR_DEV = 12
N_GX = 2
N_GY = 4
N_GZ = 4


box_side = 3.0


def draw_shape_coef(key, part):
    key = jax.random.fold_in(key, 5)
    full_shape = (N_GX, N_GY, N_GZ, V_DEV, 3, NC)
    subkeys = jax.random.split(key, 3)
    component = lax.broadcasted_iota(jnp.int32, full_shape, 4)
    coef_index = lax.broadcasted_iota(jnp.int32, full_shape, 5)
    along_x = lax.broadcasted_iota(jnp.int32, full_shape, 0)
    along_y = lax.broadcasted_iota(jnp.int32, full_shape, 1)
    along_z = lax.broadcasted_iota(jnp.int32, full_shape, 2)
    cell_coord = jnp.where(component == 0, along_x, jnp.where(component == 1, along_y, along_z)).astype(jnp.float32)
    degree = np.floor(np.sqrt(np.arange(NC) + 0.5))
    damping = jnp.asarray(1.0 / np.maximum(degree - 1.0, 1.0), dtype=jnp.float32)
    offset = jax.random.uniform(subkeys[0], (N_GX, N_GY, N_GZ, V_DEV, 3, 1), jnp.float32, 0.25, 0.75)
    radius = jax.random.uniform(subkeys[1], (N_GX, N_GY, N_GZ, V_DEV, 1, 1), jnp.float32, 0.85, 1.15)
    roughness = 0.1 * jax.random.normal(subkeys[2], full_shape, jnp.float32)
    center = (cell_coord + offset) * box_side
    unit_slot = jnp.where(component == 0, 3, jnp.where(component == 1, 1, 2))
    coefficients = jnp.where(coef_index == 0, center * (2.0 * math.sqrt(math.pi)), 0.0)
    coefficients = coefficients + jnp.where(coef_index == unit_slot, radius * math.sqrt(4.0 * math.pi / 3.0), 0.0)
    coefficients = coefficients + jnp.where(coef_index >= 4, roughness * damping, 0.0)
    return coefficients.astype(jnp.float32)


def draw_pair_count(key, part):
    key = jax.random.fold_in(key, 12)
    subkeys = jax.random.split(key, 2)
    spread = jax.random.randint(subkeys[0], (N_GX, N_GY, N_GZ), 0, 2 * V_DEV + 1)
    counts = V_DEV + spread * spread // (2 * V_DEV)
    chosen = jax.random.randint(subkeys[1], (), 0, N_GX * N_GY * N_GZ)
    flat_index = lax.broadcasted_iota(jnp.int32, (N_GX * N_GY * N_GZ,), 0).reshape(N_GX, N_GY, N_GZ)
    return jnp.where(flat_index == chosen, PAIR_DEV, counts).astype(jnp.int32)


def draw_pair_slots(key, part):
    key = jax.random.fold_in(key, 11)
    full_shape = (N_GX, N_GY, N_GZ, PAIR_DEV)
    subkeys = jax.random.split(key, 11)
    along_x = lax.broadcasted_iota(jnp.int32, full_shape, 0)
    along_y = lax.broadcasted_iota(jnp.int32, full_shape, 1)
    along_z = lax.broadcasted_iota(jnp.int32, full_shape, 2)
    slot_index = lax.broadcasted_iota(jnp.int32, full_shape, 3)

    def neighbour_step(subkey, coord, extent):
        shift_value = jax.random.randint(subkey, full_shape, -1, 2)
        moved = coord + shift_value
        return jnp.where((moved < 0) | (moved >= extent), -shift_value, shift_value)
    step_x = neighbour_step(subkeys[0], along_x, N_GX)
    step_y = neighbour_step(subkeys[1], along_y, N_GY)
    step_z = neighbour_step(subkeys[2], along_z, N_GZ)
    first_local = jax.random.randint(subkeys[3], full_shape, 0, V_DEV)
    first_local = jnp.where(slot_index < V_DEV, slot_index, first_local)
    second_local = jax.random.randint(subkeys[4], full_shape, 0, V_DEV)
    coincide = (step_x == 0) & (step_y == 0) & (step_z == 0) & (second_local == first_local)
    second_local = jnp.where(coincide, (second_local + 1) % V_DEV, second_local)
    offset_code = (step_x + 1) * 9 + (step_y + 1) * 3 + (step_z + 1)
    second_entry = offset_code * V_DEV + second_local
    first_entry = 13 * V_DEV + first_local
    upper_x = jax.random.randint(subkeys[5], (), 0, N_GX - 1)
    upper_y = jax.random.randint(subkeys[6], (), 0, N_GY - 1)
    upper_z = jax.random.randint(subkeys[7], (), 0, N_GZ - 1)
    upper_corner = (along_x == upper_x) & (along_y == upper_y) & (along_z == upper_z) & (slot_index == 0)
    second_entry = jnp.where(upper_corner, 27 * V_DEV - 1, second_entry)
    lower_x = jax.random.randint(subkeys[8], (), 1, N_GX)
    lower_y = jax.random.randint(subkeys[9], (), 1, N_GY)
    lower_z = jax.random.randint(subkeys[10], (), 1, N_GZ)
    lower_corner = (along_x == lower_x) & (along_y == lower_y) & (along_z == lower_z) & (slot_index == 1)
    second_entry = jnp.where(lower_corner, 0, second_entry)
    return jnp.stack([first_entry, second_entry], axis=-1).astype(jnp.int32)


def levels(own_key, shape, pieces, least, top_value):
    gain = 1.0
    for axis_at, parts in pieces:
        heights = jax.random.uniform(jax.random.fold_in(jax.random.fold_in(own_key, 6), axis_at), (parts,), jnp.float32, least / len(pieces), top_value / len(pieces))
        gain = gain * jnp.repeat(jnp.exp(heights), shape[axis_at] // parts).reshape((-1,) + (1,) * (len(shape) - 1 - axis_at))
    return gain


def bell_draw(stream_key, dims, scale, limit, cuts=(), kind=jnp.bfloat16):
    values = jax.random.normal(stream_key, dims, jnp.float32) * scale
    if len(cuts) > 0:
        values = levels(stream_key, dims, cuts, -0.22, 0.18) * values
    return jnp.clip(values, min=-limit, max=limit).astype(kind)


def setup_inputs(seed: int = 0) -> dict:
    seeds = jax.random.split(jax.random.key(seed), 5)
    shape_coef = draw_shape_coef(jax.random.fold_in(seeds[4], 71), 0)
    density_coef = bell_draw(seeds[1], (N_GX, N_GY, N_GZ, V_DEV, 3, NC), 0.3, 1.8, ((0, 2), (1, 4), (2, 4)), jnp.float32)
    pair_count = draw_pair_count(jax.random.fold_in(seeds[4], 71), 0)
    pair_slots = draw_pair_slots(jax.random.fold_in(seeds[4], 71), 0)
    return dict(shape_coef=shape_coef, density_coef=density_coef, pair_count=pair_count, pair_slots=pair_slots)


blob_radius = 0.25

def gauss_nodes(node_count):
    numbers = np.arange(1, node_count + 1)
    cosine = np.cos(np.pi * (numbers - 0.25) / (node_count + 0.5))

    def legendre_pair(points):
        legendre_prev = np.ones(points.shape)
        legendre_next = np.array(points)
        for degree in range(2, node_count + 1):
            legendre_prev, legendre_next = (legendre_next, ((2.0 * degree - 1.0) * points * legendre_next - (degree - 1.0) * legendre_prev) / degree)
        slope = node_count * (points * legendre_next - legendre_prev) / (points * points - 1.0)
        return (legendre_next, slope)
    for newton_step in range(100):
        value_now, slope = legendre_pair(cosine)
        cosine = cosine - value_now / slope
    value_now, slope = legendre_pair(cosine)
    weights = 2.0 / ((1.0 - cosine * cosine) * slope * slope)
    return (np.array(cosine[::-1]), np.array(weights[::-1]))

def harmonic_table(top_degree, latitudes, longitudes):
    cosine, gauss_weight = gauss_nodes(latitudes)
    sine_theta = np.sqrt(1.0 - cosine * cosine)
    angles = 2.0 * np.pi * np.arange(longitudes) / longitudes
    legendre = np.zeros((top_degree + 1, top_degree + 1, latitudes))
    legendre[0, 0] = np.sqrt(0.25 / np.pi)
    for degree_m in range(1, top_degree + 1):
        legendre[degree_m, degree_m] = np.sqrt((2.0 * degree_m + 1.0) / (2.0 * degree_m)) * sine_theta * legendre[degree_m - 1, degree_m - 1]
    for degree_m in range(top_degree + 1):
        if degree_m + 1 <= top_degree:
            legendre[degree_m + 1, degree_m] = np.sqrt(2.0 * degree_m + 3.0) * cosine * legendre[degree_m, degree_m]
        for degree_l in range(degree_m + 2, top_degree + 1):
            factor = np.sqrt((4.0 * degree_l * degree_l - 1.0) / (degree_l * degree_l - degree_m * degree_m))
            lagged = np.sqrt(((degree_l - 1.0) * (degree_l - 1.0) - degree_m * degree_m) / (4.0 * (degree_l - 1.0) * (degree_l - 1.0) - 1.0))
            legendre[degree_l, degree_m] = factor * (cosine * legendre[degree_l - 1, degree_m] - lagged * legendre[degree_l - 2, degree_m])
    table_rows = []
    for degree_l in range(top_degree + 1):
        for signed in range(-degree_l, degree_l + 1):
            polar_part = legendre[degree_l, abs(signed)][:, None]
            if signed > 0:
                azimuth = np.sqrt(2.0) * np.cos(signed * angles)
            elif signed < 0:
                azimuth = np.sqrt(2.0) * np.sin(-signed * angles)
            else:
                azimuth = np.ones(longitudes)
            table_rows.append((polar_part * azimuth[None, :]).reshape(-1))
    synthesis = np.stack(table_rows)
    weights = np.repeat(gauss_weight, longitudes) * (2.0 * np.pi / longitudes)
    return (synthesis, weights)

def grid_tables():
    target_synth, target_weight = harmonic_table(P_SIZE, P_SIZE + 1, 2 * (P_SIZE + 1))
    upsample_synth, upsample_weight = harmonic_table(P_SIZE, Q + 1, 2 * (Q + 1))
    analysis = (target_synth * target_weight[None, :]).T
    return (jnp.asarray(target_synth, dtype=jnp.float32), jnp.asarray(upsample_synth, dtype=jnp.float32), jnp.asarray(upsample_weight, dtype=jnp.float32), jnp.asarray(analysis, dtype=jnp.float32))

def surface_grids(shape_part, density_part, tables):
    target_synth, upsample_synth, upsample_weight, analysis = tables
    targets = jnp.einsum('nck,kt->nct', shape_part, target_synth, precision=lax.Precision.HIGHEST)
    sources = jnp.einsum('nck,kt->nct', shape_part, upsample_synth, precision=lax.Precision.HIGHEST)
    weighted = jnp.einsum('nck,kt->nct', density_part, upsample_synth, precision=lax.Precision.HIGHEST) * upsample_weight
    return jnp.concatenate([targets, sources, weighted], axis=2)

def stokes_velocity(targets, sources, weighted):
    separation = targets[:, :, None] - sources[:, None, :]
    squared = lax.optimization_barrier(jnp.sum(separation * separation, axis=0))
    softened = squared + blob_radius * blob_radius
    inverse = lax.rsqrt(softened)
    inverse_cube = inverse * inverse * inverse
    projected = lax.optimization_barrier(jnp.sum(separation * weighted[:, None, :], axis=0))
    kernel_terms = ((softened + blob_radius * blob_radius) * weighted[:, None, :] + projected * separation) * inverse_cube
    return lax.optimization_barrier(jnp.sum(kernel_terms, axis=2)) * (0.125 / math.pi)

def pair_velocity(first_grid, second_grid, target_count, source_count):
    edge = target_count + source_count
    first_velocity = stokes_velocity(first_grid[:, :target_count], second_grid[:, target_count:edge], second_grid[:, edge:])
    second_velocity = stokes_velocity(second_grid[:, :target_count], first_grid[:, target_count:edge], first_grid[:, edge:])
    return (first_velocity, second_velocity)

def reference(shape_coef, density_coef, pair_count, pair_slots):
    tables = grid_tables()
    target_count = 2 * (P_SIZE + 1) * (P_SIZE + 1)
    source_count = 2 * (Q + 1) * (Q + 1)
    devices_all = N_GX * N_GY * N_GZ
    vesicles_all = devices_all * V_DEV
    surface = surface_grids(shape_coef.reshape(vesicles_all, 3, NC), density_coef.reshape(vesicles_all, 3, NC), tables)
    owners = jnp.arange(devices_all, dtype=jnp.int32)
    owner_x = owners // (N_GY * N_GZ)
    owner_y = owners // N_GZ % N_GY
    owner_z = owners % N_GZ
    entries = pair_slots.reshape(devices_all, PAIR_DEV, 2).astype(jnp.int32)

    def global_ident(entry):
        near_x = owner_x[:, None] + entry // (9 * V_DEV) - 1
        near_y = owner_y[:, None] + entry // (3 * V_DEV) % 3 - 1
        near_z = owner_z[:, None] + entry // V_DEV % 3 - 1
        return (((near_x * N_GY + near_y) * N_GZ + near_z) * V_DEV + entry % V_DEV).reshape(-1).astype(jnp.int32)
    first_ids = global_ident(entries[:, :, 0])
    second_ids = global_ident(entries[:, :, 1])
    active = (jnp.arange(PAIR_DEV, dtype=jnp.int32)[None, :] < pair_count.reshape(devices_all, 1)).reshape(-1)

    def evaluate(pair_item):
        first_id, second_id, usable = pair_item

        def compute():
            return pair_velocity(surface[first_id], surface[second_id], target_count, source_count)

        def vacant():
            blank_rows = jnp.zeros((3, target_count), jnp.float32)
            return (blank_rows, blank_rows)
        return lax.cond(usable, compute, vacant)
    first_velocity, second_velocity = lax.map(evaluate, (first_ids, second_ids, active))
    velocity = jax.ops.segment_sum(first_velocity, first_ids, num_segments=vesicles_all)
    velocity = velocity + jax.ops.segment_sum(second_velocity, second_ids, num_segments=vesicles_all)
    result = jnp.einsum('nct,tk->nck', velocity, tables[3], precision=lax.Precision.HIGHEST)
    return result.reshape(N_GX, N_GY, N_GZ, V_DEV, 3, NC)
```

```python
import functools
import itertools
import math

import jax
import jax.numpy as jnp
import numpy as np
from jax import lax
from jax.experimental import pallas as pl
from jax.experimental.pallas import tpu as pltpu
from jax.sharding import PartitionSpec as P

P_SIZE = 12
Q = 24


blob_radius = 0.25

def gauss_nodes(node_count):
    numbers = np.arange(1, node_count + 1)
    cosine = np.cos(np.pi * (numbers - 0.25) / (node_count + 0.5))

    def legendre_pair(points):
        legendre_prev = np.ones(points.shape)
        legendre_next = np.array(points)
        for degree in range(2, node_count + 1):
            legendre_prev, legendre_next = (
                legendre_next,
                ((2.0 * degree - 1.0) * points * legendre_next - (degree - 1.0) * legendre_prev)
                / degree,
            )
        slope = node_count * (points * legendre_next - legendre_prev) / (points * points - 1.0)
        return (legendre_next, slope)

    for newton_step in range(100):
        value_now, slope = legendre_pair(cosine)
        cosine = cosine - value_now / slope
    value_now, slope = legendre_pair(cosine)
    weights = 2.0 / ((1.0 - cosine * cosine) * slope * slope)
    return (np.array(cosine[::-1]), np.array(weights[::-1]))


def harmonic_table(top_degree, latitudes, longitudes):
    cosine, gauss_weight = gauss_nodes(latitudes)
    sine_theta = np.sqrt(1.0 - cosine * cosine)
    angles = 2.0 * np.pi * np.arange(longitudes) / longitudes
    legendre = np.zeros((top_degree + 1, top_degree + 1, latitudes))
    legendre[0, 0] = np.sqrt(0.25 / np.pi)
    for degree_m in range(1, top_degree + 1):
        legendre[degree_m, degree_m] = (
            np.sqrt((2.0 * degree_m + 1.0) / (2.0 * degree_m))
            * sine_theta
            * legendre[degree_m - 1, degree_m - 1]
        )
    for degree_m in range(top_degree + 1):
        if degree_m + 1 <= top_degree:
            legendre[degree_m + 1, degree_m] = (
                np.sqrt(2.0 * degree_m + 3.0) * cosine * legendre[degree_m, degree_m]
            )
        for degree_l in range(degree_m + 2, top_degree + 1):
            factor = np.sqrt(
                (4.0 * degree_l * degree_l - 1.0) / (degree_l * degree_l - degree_m * degree_m)
            )
            lagged = np.sqrt(
                ((degree_l - 1.0) * (degree_l - 1.0) - degree_m * degree_m)
                / (4.0 * (degree_l - 1.0) * (degree_l - 1.0) - 1.0)
            )
            legendre[degree_l, degree_m] = factor * (
                cosine * legendre[degree_l - 1, degree_m]
                - lagged * legendre[degree_l - 2, degree_m]
            )
    table_rows = []
    for degree_l in range(top_degree + 1):
        for signed in range(-degree_l, degree_l + 1):
            polar_part = legendre[degree_l, abs(signed)][:, None]
            if signed > 0:
                azimuth = np.sqrt(2.0) * np.cos(signed * angles)
            elif signed < 0:
                azimuth = np.sqrt(2.0) * np.sin(-signed * angles)
            else:
                azimuth = np.ones(longitudes)
            table_rows.append((polar_part * azimuth[None, :]).reshape(-1))
    synthesis = np.stack(table_rows)
    weights = np.repeat(gauss_weight, longitudes) * (2.0 * np.pi / longitudes)
    return (synthesis, weights)

AXES = ("gx", "gy", "gz")
OFFSETS = list(itertools.product((-1, 0, 1), repeat=3))
HEAD = 128
T_PAD = 384
T_ROWS = 352
S_PAD = 1280
CHUNK = 256
SUB = 32
COLS = 16


def split_table(table):
    high = table.astype(np.float32).astype(jnp.bfloat16)
    low = (table - high.astype(np.float64)).astype(jnp.bfloat16)
    pad = np.zeros((512 - 3 * table.shape[0], table.shape[1]), jnp.bfloat16)
    return np.concatenate(
        [high[:HEAD], low[:HEAD], high[:HEAD], high[HEAD:], low[HEAD:], high[HEAD:], pad]
    )


def grid_tables():
    target_synth, target_weight = harmonic_table(P_SIZE, P_SIZE + 1, 2 * (P_SIZE + 1))
    upsample_synth, upsample_weight = harmonic_table(P_SIZE, Q + 1, 2 * (Q + 1))
    targets, sources = target_synth.shape[1], upsample_synth.shape[1]
    target_wide = np.pad(target_synth, ((0, 0), (0, T_PAD - targets)))
    source_wide = np.pad(upsample_synth, ((0, 0), (0, S_PAD - sources)))
    weight_row = np.pad(upsample_weight, (0, S_PAD - sources))[None, :]
    analysis = np.pad(
        (target_synth * target_weight[None, :]).T,
        ((0, T_PAD - targets), (0, 256 - target_synth.shape[0])),
    )
    return (
        jnp.asarray(split_table(source_wide)),
        jnp.asarray(np.ascontiguousarray(split_table(target_wide).T)),
        jnp.asarray(weight_row, dtype=jnp.float32),
        jnp.asarray(analysis, dtype=jnp.float32),
    )


def halo_kernel(sizes, own_ref, out_ref, send_sem, recv_sem):
    here = [lax.axis_index(axis) for axis in AXES]

    def place(offset):
        there = [h + o for h, o in zip(here, offset)]
        exists = None
        for spot, o, size in zip(there, offset, sizes):
            if o:
                inside = (spot >= 0) & (spot < size)
                exists = inside if exists is None else exists & inside
        return tuple(there), exists

    barrier = pltpu.get_barrier_semaphore()
    around = 1
    for h, size in zip(here, sizes):
        around = around * (1 + (h > 0).astype(jnp.int32) + (h < size - 1).astype(jnp.int32))
    for offset in OFFSETS:
        if any(offset):
            there, exists = place(offset)

            @pl.when(exists)
            def _():
                pl.semaphore_signal(
                    barrier, inc=1, device_id=there, device_id_type=pl.DeviceIdType.MESH
                )

    pl.semaphore_wait(barrier, around - 1)

    def transfer(code):
        there, exists = place(OFFSETS[code])
        copy = pltpu.make_async_remote_copy(
            src_ref=own_ref,
            dst_ref=out_ref.at[26 - code],
            send_sem=send_sem.at[code],
            recv_sem=recv_sem.at[26 - code],
            device_id=there,
            device_id_type=pl.DeviceIdType.MESH,
        )
        return copy, exists

    for code in range(27):
        if code != 13:
            copy, exists = transfer(code)

            @pl.when(exists)
            def _():
                copy.start()

    out_ref[13] = own_ref[...]
    for code in range(27):
        if code != 13:
            there, exists = place(OFFSETS[code])

            @pl.when(jnp.logical_not(exists))
            def _():
                out_ref[code] = jnp.zeros(own_ref.shape, jnp.float32)

    for code in range(27):
        if code != 13:
            there, exists = place(OFFSETS[code])

            @pl.when(exists)
            def _():
                copy = pltpu.make_async_remote_copy(
                    src_ref=own_ref,
                    dst_ref=out_ref.at[code],
                    send_sem=send_sem.at[code],
                    recv_sem=recv_sem.at[code],
                    device_id=there,
                    device_id_type=pl.DeviceIdType.MESH,
                )
                copy.wait()


def halo(packed, sizes):
    return pl.pallas_call(
        functools.partial(halo_kernel, sizes),
        out_shape=jax.ShapeDtypeStruct((27,) + packed.shape, jnp.float32),
        in_specs=[pl.BlockSpec(memory_space=pltpu.VMEM)],
        out_specs=pl.BlockSpec(memory_space=pltpu.VMEM),
        scratch_shapes=[pltpu.SemaphoreType.DMA((27,)), pltpu.SemaphoreType.DMA((27,))],
        compiler_params=pltpu.CompilerParams(collective_id=0, has_side_effects=True),
        name="halo",
    )(packed)


NT = (((1,), (1,)), ((), ()))


def near_kernel(
    names_ref, packed_ref, source_table, target_table, weight_ref, analysis_ref, out_ref,
    coef, grids, centre, spread, totals, columns, high, low, target_list, source_list,
):
    delta2 = blob_radius * blob_radius
    lanes = lax.broadcasted_iota(jnp.int32, (27, 8, HEAD), 2)
    rows8 = lax.broadcasted_iota(jnp.int32, (27, 8, HEAD), 1)
    tails = packed_ref[:, 24:32, :]
    for group in range(3):
        head = packed_ref[:, 8 * group : 8 * group + 8, :]
        centre[:, 8 * group : 8 * group + 8, :] = jnp.broadcast_to(
            head[:, :, 0:1] * (0.5 / math.sqrt(math.pi)), head.shape
        )
        head = jnp.where((lanes == 0) & (rows8 + 8 * group < 12), 0.0, head)
        head_high = head.astype(jnp.bfloat16).astype(jnp.float32)
        tail = tails if group == 0 else pltpu.roll(tails, HEAD - 41 * group, 2)
        tail = jnp.where(lanes < 41, tail, 0.0)
        tail_high = tail.astype(jnp.bfloat16).astype(jnp.float32)
        tail_low = tail - tail_high
        rows = slice(8 * group, 8 * group + 8)
        coef[:, rows, 0:128] = head_high
        coef[:, rows, 128:256] = head_high
        coef[:, rows, 256:384] = head - head_high
        coef[:, rows, 384:512] = (
            tail_high + pltpu.roll(tail_high, 41, 2) + pltpu.roll(tail_low, 82, 2)
        )

    own = coef[13].astype(jnp.bfloat16)
    column_points = lax.dot_general(
        target_table[0:T_ROWS, :], own, NT, preferred_element_type=jnp.float32
    )
    for row in range(12):
        spread[row] = jnp.broadcast_to(column_points[:, row : row + 1], (T_ROWS, HEAD))
    row_points = lax.dot_general(own, target_table[...], NT, preferred_element_type=jnp.float32)

    everything = coef[...].reshape(27 * 24, 512).astype(jnp.bfloat16)

    @pl.loop(0, S_PAD // CHUNK)
    def _(step):
        span = pl.ds(pl.multiple_of(step * CHUNK, CHUNK), CHUNK)
        grids[:, span] = jnp.dot(
            everything, source_table[:, span], preferred_element_type=jnp.float32
        )

    def scan_device(code, filled):
        def scan_slot(slot, filled):
            first = names_ref[code, 2 * slot]
            second = names_ref[code, 2 * slot + 1]
            target_list[filled] = second & 3
            source_list[filled] = code * 4 + (first & 3)
            return filled + ((second >> 2) == 26 - code).astype(jnp.int32)

        return lax.fori_loop(0, names_ref[code, 24], scan_slot, filled)

    def own_slot(slot, filled):
        target_list[filled] = names_ref[13, 2 * slot] & 3
        source_list[filled] = names_ref[13, 2 * slot + 1]
        return filled + 1

    filled = lax.fori_loop(0, 27, scan_device, 0)
    filled = lax.fori_loop(0, names_ref[13, 24], own_slot, filled)

    totals[...] = jnp.zeros(totals.shape, jnp.float32)

    @pl.loop(0, filled)
    def _(item):
        target = target_list[item]
        entry = source_list[item]
        device = entry >> 2
        vesicle = entry & 3
        base = device * 24 + vesicle * 3
        weight = weight_ref[...]
        points, forces = [], []
        for i in range(3):
            moved = centre[device, pl.ds(vesicle * 3 + i, 1), :] - centre[13, pl.ds(target * 3 + i, 1), :]
            points.append(grids[pl.ds(base + i, 1), :] + jnp.concatenate([moved] * (S_PAD // HEAD), axis=1))
            forces.append(grids[pl.ds(base + 12 + i, 1), :] * weight)
        square = points[0] * points[0] + points[1] * points[1] + points[2] * points[2] + 2.0 * delta2
        along = points[0] * forces[0] + points[1] * forces[1] + points[2] * forces[2]
        for i in range(3):
            columns[i : i + 1, :] = forces[i]
            for j in range(3):
                columns[3 + 3 * i + j : 4 + 3 * i + j, :] = forces[i] * points[j]
            columns[12 + i : 13 + i, :] = square * forces[i] + along * points[i]
        wide = columns[...]
        wide_high = wide.astype(jnp.bfloat16)
        wide_low = (wide - wide_high.astype(jnp.float32)).astype(jnp.bfloat16)
        both = jnp.concatenate([wide_high, wide_low], axis=0)
        total = None
        for step in range(S_PAD // CHUNK):
            span = slice(step * CHUNK, (step + 1) * CHUNK)
            near = [jnp.broadcast_to(point[:, span], (SUB, CHUNK)) for point in points]
            for part in range(T_ROWS // SUB):
                rows = slice(part * SUB, (part + 1) * SUB)
                softened = None
                for i in range(3):
                    x = spread[target * 3 + i, rows, :]
                    gap = jnp.concatenate([x] * (CHUNK // HEAD), axis=1) - near[i]
                    softened = gap * gap + (delta2 if softened is None else softened)
                inverse = lax.rsqrt(softened)
                cube = inverse * inverse * inverse
                cube_high = cube.astype(jnp.bfloat16)
                high[step, rows, :] = cube_high
                low[step, rows, :] = (cube - cube_high.astype(jnp.float32)).astype(jnp.bfloat16)
            term = lax.dot_general(
                high[step], both[:, span], NT, preferred_element_type=jnp.float32
            ) + lax.dot_general(low[step], both[:, span], NT, preferred_element_type=jnp.float32)
            total = term if total is None else total + term
        totals[target, 0:T_ROWS, 0 : 2 * COLS] += total

    for vesicle in range(4):
        turned = jnp.transpose(totals[vesicle])
        sums = turned[0:COLS] + turned[COLS : 2 * COLS]
        x = [row_points[3 * vesicle + i : 3 * vesicle + i + 1, :] for i in range(3)]
        plain = [sums[i : i + 1, :] for i in range(3)]
        cross = [[sums[3 + 3 * i + j : 4 + 3 * i + j, :] for j in range(3)] for i in range(3)]
        last = [sums[12 + i : 13 + i, :] for i in range(3)]
        square = x[0] * x[0] + x[1] * x[1] + x[2] * x[2]
        along = x[0] * plain[0] + x[1] * plain[1] + x[2] * plain[2]
        trace = cross[0][0] + cross[1][1] + cross[2][2]
        for i in range(3):
            value = square * plain[i] + x[i] * (along - trace) + last[i]
            for j in range(3):
                value = value - x[j] * (2.0 * cross[i][j] + cross[j][i])
            columns[3 * vesicle + i : 3 * vesicle + i + 1, 0:T_PAD] = value * (0.125 / math.pi)
    out_ref[...] = jnp.dot(
        columns[0:16, 0:T_PAD],
        analysis_ref[...],
        precision=lax.Precision.HIGHEST,
        preferred_element_type=jnp.float32,
    )


def near(names, packed, tables):
    vmem = pl.BlockSpec(memory_space=pltpu.VMEM)
    return pl.pallas_call(
        near_kernel,
        out_shape=jax.ShapeDtypeStruct((16, 256), jnp.float32),
        in_specs=[pl.BlockSpec(memory_space=pltpu.SMEM)] + [vmem] * 5,
        out_specs=vmem,
        scratch_shapes=[
            pltpu.VMEM((27, 24, 512), jnp.float32),
            pltpu.VMEM((27 * 24, S_PAD), jnp.float32),
            pltpu.VMEM((27, 24, HEAD), jnp.float32),
            pltpu.VMEM((12, T_ROWS, HEAD), jnp.float32),
            pltpu.VMEM((4, T_PAD, HEAD), jnp.float32),
            pltpu.VMEM((COLS, S_PAD), jnp.float32),
            pltpu.VMEM((S_PAD // CHUNK, T_ROWS, CHUNK), jnp.bfloat16),
            pltpu.VMEM((S_PAD // CHUNK, T_ROWS, CHUNK), jnp.bfloat16),
            pltpu.SMEM((360,), jnp.int32),
            pltpu.SMEM((360,), jnp.int32),
        ],
        compiler_params=pltpu.CompilerParams(vmem_limit_bytes=48 * 1024 * 1024),
        name="near",
    )(names, packed, *tables)


def on_device(sizes, shape_coef, density_coef, pair_count, pair_slots):
    coefficients = jnp.concatenate(
        [shape_coef.reshape(12, -1), density_coef.reshape(12, -1)], axis=0
    )
    names = jnp.concatenate(
        [pair_slots.reshape(24), pair_count.reshape(1), jnp.zeros((15,), jnp.int32)]
    ).astype(jnp.float32)
    tails = coefficients[:, HEAD:]
    tails = jnp.concatenate(
        [tails[0:8], tails[8:16], tails[16:24], names.reshape(8, 5)], axis=1
    )
    packed = jnp.concatenate([coefficients[:, :HEAD], tails], axis=0)
    packed = halo(packed, sizes)
    names = packed[:, 24:, 123:].reshape(27, 40).astype(jnp.int32)
    result = near(names, packed, grid_tables())
    return result[:12, : shape_coef.shape[-1]].reshape(shape_coef.shape)


def solution(mesh):
    placed = (
        P("gx", "gy", "gz", None, None, None),
        P("gx", "gy", "gz", None, None, None),
        P("gx", "gy", "gz"),
        P("gx", "gy", "gz", None, None),
    )
    return jax.shard_map(
        functools.partial(on_device, tuple(mesh.shape[axis] for axis in AXES)),
        mesh=mesh,
        in_specs=placed,
        out_specs=P("gx", "gy", "gz", None, None, None),
        check_vma=False,
    )
```

```python
import functools
import itertools
import math

import jax
import jax.numpy as jnp
import numpy as np
from jax import lax
from jax.experimental import pallas as pl
from jax.experimental.pallas import tpu as pltpu
from jax.sharding import PartitionSpec as P

P_SIZE = 12
Q = 24


blob_radius = 0.25

def gauss_nodes(node_count):
    numbers = np.arange(1, node_count + 1)
    cosine = np.cos(np.pi * (numbers - 0.25) / (node_count + 0.5))

    def legendre_pair(points):
        legendre_prev = np.ones(points.shape)
        legendre_next = np.array(points)
        for degree in range(2, node_count + 1):
            legendre_prev, legendre_next = (
                legendre_next,
                ((2.0 * degree - 1.0) * points * legendre_next - (degree - 1.0) * legendre_prev)
                / degree,
            )
        slope = node_count * (points * legendre_next - legendre_prev) / (points * points - 1.0)
        return (legendre_next, slope)

    for newton_step in range(100):
        value_now, slope = legendre_pair(cosine)
        cosine = cosine - value_now / slope
    value_now, slope = legendre_pair(cosine)
    weights = 2.0 / ((1.0 - cosine * cosine) * slope * slope)
    return (np.array(cosine[::-1]), np.array(weights[::-1]))


def harmonic_table(top_degree, latitudes, longitudes):
    cosine, gauss_weight = gauss_nodes(latitudes)
    sine_theta = np.sqrt(1.0 - cosine * cosine)
    angles = 2.0 * np.pi * np.arange(longitudes) / longitudes
    legendre = np.zeros((top_degree + 1, top_degree + 1, latitudes))
    legendre[0, 0] = np.sqrt(0.25 / np.pi)
    for degree_m in range(1, top_degree + 1):
        legendre[degree_m, degree_m] = (
            np.sqrt((2.0 * degree_m + 1.0) / (2.0 * degree_m))
            * sine_theta
            * legendre[degree_m - 1, degree_m - 1]
        )
    for degree_m in range(top_degree + 1):
        if degree_m + 1 <= top_degree:
            legendre[degree_m + 1, degree_m] = (
                np.sqrt(2.0 * degree_m + 3.0) * cosine * legendre[degree_m, degree_m]
            )
        for degree_l in range(degree_m + 2, top_degree + 1):
            factor = np.sqrt(
                (4.0 * degree_l * degree_l - 1.0) / (degree_l * degree_l - degree_m * degree_m)
            )
            lagged = np.sqrt(
                ((degree_l - 1.0) * (degree_l - 1.0) - degree_m * degree_m)
                / (4.0 * (degree_l - 1.0) * (degree_l - 1.0) - 1.0)
            )
            legendre[degree_l, degree_m] = factor * (
                cosine * legendre[degree_l - 1, degree_m]
                - lagged * legendre[degree_l - 2, degree_m]
            )
    table_rows = []
    for degree_l in range(top_degree + 1):
        for signed in range(-degree_l, degree_l + 1):
            polar_part = legendre[degree_l, abs(signed)][:, None]
            if signed > 0:
                azimuth = np.sqrt(2.0) * np.cos(signed * angles)
            elif signed < 0:
                azimuth = np.sqrt(2.0) * np.sin(-signed * angles)
            else:
                azimuth = np.ones(longitudes)
            table_rows.append((polar_part * azimuth[None, :]).reshape(-1))
    synthesis = np.stack(table_rows)
    weights = np.repeat(gauss_weight, longitudes) * (2.0 * np.pi / longitudes)
    return (synthesis, weights)

AXES = ("gx", "gy", "gz")
OFFSETS = list(itertools.product((-1, 0, 1), repeat=3))
HEAD = 128
TAIL = 41
MESSAGE = 40
T_PAD = 384
T_ROWS = 352
S_PAD = 1280
CHUNK = 1280
COLS = 16


def split_table(table):
    high = table.astype(np.float32).astype(jnp.bfloat16)
    low = (table - high.astype(np.float64)).astype(jnp.bfloat16)
    pad = np.zeros((512 - 3 * table.shape[0], table.shape[1]), jnp.bfloat16)
    return np.concatenate(
        [high[:HEAD], low[:HEAD], high[:HEAD], high[HEAD:], low[HEAD:], high[HEAD:], pad]
    )


def grid_tables():
    target_synth, target_weight = harmonic_table(P_SIZE, P_SIZE + 1, 2 * (P_SIZE + 1))
    upsample_synth, upsample_weight = harmonic_table(P_SIZE, Q + 1, 2 * (Q + 1))
    targets, sources = target_synth.shape[1], upsample_synth.shape[1]
    target_wide = np.pad(target_synth, ((0, 0), (0, T_PAD - targets)))
    source_wide = np.pad(upsample_synth, ((0, 0), (0, S_PAD - sources)))
    weight_rows = np.pad(upsample_weight, (0, S_PAD - sources)).reshape(-1, 256)
    weight_rows = np.pad(weight_rows, ((0, 8 - weight_rows.shape[0]), (0, 0)))
    analysis = np.pad(
        (target_synth * target_weight[None, :]).T,
        ((0, T_PAD - targets), (0, 256 - target_synth.shape[0])),
    )
    return (
        jnp.asarray(split_table(source_wide)),
        jnp.asarray(np.ascontiguousarray(split_table(target_wide).T)),
        jnp.asarray(np.concatenate([analysis, weight_rows]), dtype=jnp.float32),
    )


def halo_kernel(
    sizes, shape_ref, density_ref, slots_ref, count_ref, out_ref, names_ref,
    own_ref, tail_ref, send_sem, recv_sem,
):
    here = [lax.axis_index(axis) for axis in AXES]

    def place(offset):
        there = [h + o for h, o in zip(here, offset)]
        exists = None
        for spot, o, size in zip(there, offset, sizes):
            if o:
                inside = (spot >= 0) & (spot < size)
                exists = inside if exists is None else exists & inside
        return tuple(there), exists

    barrier = pltpu.get_barrier_semaphore()
    around = 1
    for h, size in zip(here, sizes):
        around = around * (1 + (h > 0).astype(jnp.int32) + (h < size - 1).astype(jnp.int32))
    for offset in OFFSETS:
        if any(offset):
            there, exists = place(offset)

            @pl.when(exists)
            def _():
                pl.semaphore_signal(
                    barrier, inc=1, device_id=there, device_id_type=pl.DeviceIdType.MESH
                )

    own_ref[32:MESSAGE, :] = jnp.zeros((MESSAGE - 32, HEAD), jnp.float32)
    tail_ref[...] = jnp.zeros(tail_ref.shape, jnp.float32)
    for start, source in ((0, shape_ref), (12, density_ref)):
        for i in range(3):
            rows = slice(start + 4 * i, start + 4 * i + 4)
            own_ref[rows, :] = source[i, :, 0:HEAD]
            tail_ref[rows, 0:TAIL] = source[i, :, HEAD : HEAD + TAIL]
    own_ref[24:32, :] = (
        tail_ref[0:8, :]
        + pltpu.roll(tail_ref[8:16, :], TAIL, 1)
        + pltpu.roll(tail_ref[16:24, :], 2 * TAIL, 1)
    )
    for i in range(2):
        own_ref[32 + i : 33 + i, 0:12] = slots_ref[i : i + 1, :].astype(jnp.float32)
    own_ref[34:35, :] = jnp.full((1, HEAD), count_ref[0, 0].astype(jnp.float32))
    pl.semaphore_wait(barrier, around - 1)

    def transfer(code):
        there, exists = place(OFFSETS[code])
        copy = pltpu.make_async_remote_copy(
            src_ref=own_ref,
            dst_ref=out_ref.at[26 - code],
            send_sem=send_sem.at[code],
            recv_sem=recv_sem.at[26 - code],
            device_id=there,
            device_id_type=pl.DeviceIdType.MESH,
        )
        return copy, exists

    for code in range(27):
        if code != 13:
            copy, exists = transfer(code)

            @pl.when(exists)
            def _():
                copy.start()

    out_ref[13] = own_ref[...]
    for code in range(27):
        if code != 13:
            there, exists = place(OFFSETS[code])

            @pl.when(jnp.logical_not(exists))
            def _():
                out_ref[code] = jnp.zeros(own_ref.shape, jnp.float32)

    for code in range(27):
        if code != 13:
            there, exists = place(OFFSETS[code])

            @pl.when(exists)
            def _():
                copy = pltpu.make_async_remote_copy(
                    src_ref=own_ref,
                    dst_ref=out_ref.at[code],
                    send_sem=send_sem.at[code],
                    recv_sem=recv_sem.at[code],
                    device_id=there,
                    device_id_type=pl.DeviceIdType.MESH,
                )
                copy.wait()

    for code in range(27):
        flat = out_ref[code, 32:MESSAGE, :].astype(jnp.int32)
        lanes = lax.broadcasted_iota(jnp.int32, (1, HEAD), 1)
        names_ref[code : code + 1, :] = jnp.where(
            lanes < 12, flat[0:1], jnp.where(lanes < 24, pltpu.roll(flat, 12, 1)[1:2], flat[2:3])
        )


def halo(shape, density, slots, count, sizes):
    vmem = pl.BlockSpec(memory_space=pltpu.VMEM)
    return pl.pallas_call(
        functools.partial(halo_kernel, sizes),
        out_shape=(
            jax.ShapeDtypeStruct((27, MESSAGE, HEAD), jnp.float32),
            jax.ShapeDtypeStruct((27, HEAD), jnp.int32),
        ),
        in_specs=[vmem, vmem, vmem, pl.BlockSpec(memory_space=pltpu.SMEM)],
        out_specs=(vmem, vmem),
        scratch_shapes=[
            pltpu.VMEM((MESSAGE, HEAD), jnp.float32),
            pltpu.VMEM((24, HEAD), jnp.float32),
            pltpu.SemaphoreType.DMA((27,)),
            pltpu.SemaphoreType.DMA((27,)),
        ],
        compiler_params=pltpu.CompilerParams(collective_id=0, has_side_effects=True),
        name="halo",
    )(shape, density, slots, count)


NT = (((1,), (1,)), ((), ()))


def split_three(value):
    first = value.astype(jnp.bfloat16).astype(jnp.float32)
    rest = value - first
    second = rest.astype(jnp.bfloat16).astype(jnp.float32)
    return first, second, rest - second


def near_kernel(
    names_ref, packed_hbm, source_hbm, target_table, analysis_ref, out_ref,
    coef, grids, centre, lifted, slab, totals, columns, target_list, source_list,
    packed_ref, source_table, copy_sem,
):
    delta2 = blob_radius * blob_radius
    packed_copy = pltpu.make_async_copy(packed_hbm, packed_ref, copy_sem.at[0])
    source_copy = pltpu.make_async_copy(source_hbm, source_table, copy_sem.at[1])
    packed_copy.start()
    source_copy.start()
    def scan_device(code, filled):
        def scan_slot(slot, filled):
            first = names_ref[code, slot]
            second = names_ref[code, 12 + slot]
            target_list[filled] = second & 3
            source_list[filled] = code * 4 + (first & 3)
            return filled + ((second >> 2) == 26 - code).astype(jnp.int32)

        return lax.fori_loop(0, names_ref[code, 24], scan_slot, filled)

    def own_slot(slot, filled):
        target_list[filled] = names_ref[13, slot] & 3
        source_list[filled] = names_ref[13, 12 + slot]
        return filled + 1

    filled = lax.fori_loop(0, 27, scan_device, 0)
    filled = lax.fori_loop(0, names_ref[13, 24], own_slot, filled)

    packed_copy.wait()
    lanes = lax.broadcasted_iota(jnp.int32, (27, 8, HEAD), 2)
    rows8 = lax.broadcasted_iota(jnp.int32, (27, 8, HEAD), 1)
    tails = packed_ref[:, 24:32, :]
    for group in range(3):
        head = packed_ref[:, 8 * group : 8 * group + 8, :]
        centre[:, 8 * group : 8 * group + 8, :] = jnp.broadcast_to(
            head[:, :, 0:1] * (0.5 / math.sqrt(math.pi)), head.shape
        )
        head = jnp.where((lanes == 0) & (rows8 + 8 * group < 12), 0.0, head)
        head_high = head.astype(jnp.bfloat16).astype(jnp.float32)
        tail = tails if group == 0 else pltpu.roll(tails, HEAD - TAIL * group, 2)
        tail = jnp.where(lanes < TAIL, tail, 0.0)
        tail_high = tail.astype(jnp.bfloat16).astype(jnp.float32)
        tail_low = tail - tail_high
        rows = slice(8 * group, 8 * group + 8)
        coef[:, rows, 0:128] = head_high
        coef[:, rows, 128:256] = head_high
        coef[:, rows, 256:384] = head - head_high
        coef[:, rows, 384:512] = (
            tail_high + pltpu.roll(tail_high, TAIL, 2) + pltpu.roll(tail_low, 2 * TAIL, 2)
        )

    own = coef[13].astype(jnp.bfloat16)
    row_points = lax.dot_general(own, target_table[...], NT, preferred_element_type=jnp.float32)

    slab[...] = jnp.zeros(slab.shape, jnp.float32)
    ones = jnp.ones((1, T_PAD), jnp.float32)
    for vesicle in range(4):
        x = [row_points[4 * i + vesicle : 4 * i + vesicle + 1, :] for i in range(3)]
        for i in range(3):
            slab[0, i : i + 1, 0:T_PAD] = x[i]
        slab[0, 3:4, 0:T_PAD] = ones
        slab[0, 4:5, 0:T_PAD] = x[0] * x[0] + x[1] * x[1] + x[2] * x[2] + delta2
        first, second, third = split_three(slab[0, :, 0:T_PAD])
        lifted[vesicle] = jnp.transpose(
            jnp.concatenate(
                [first, first, second, second, first, third]
                + [jnp.zeros((HEAD - 48, T_PAD), jnp.float32)]
            )
        ).astype(jnp.bfloat16)
    for copy in range(2):
        slab[copy, 4:5, :] = jnp.ones((1, S_PAD), jnp.float32)

    source_copy.wait()
    everything = coef[...].reshape(27 * 24, 512).astype(jnp.bfloat16)

    @pl.loop(0, S_PAD // CHUNK)
    def _(step):
        span = pl.ds(pl.multiple_of(step * CHUNK, CHUNK), CHUNK)
        grids[:, span] = jnp.dot(
            everything, source_table[:, span], preferred_element_type=jnp.float32
        )

    weight = jnp.concatenate(
        [analysis_ref[T_PAD + i : T_PAD + i + 1, :] for i in range(S_PAD // 256)], axis=1
    )
    totals[...] = jnp.zeros(totals.shape, jnp.float32)

    def process(item, columns, slab):
        target = target_list[item]
        entry = source_list[item]
        device = entry >> 2
        vesicle = entry & 3
        base = device * 24 + vesicle
        points, forces = [], []
        for i in range(3):
            moved = centre[device, pl.ds(4 * i + vesicle, 1), :] - centre[13, pl.ds(4 * i + target, 1), :]
            points.append(grids[pl.ds(base + 4 * i, 1), :] + jnp.concatenate([moved] * (S_PAD // HEAD), axis=1))
            forces.append(grids[pl.ds(base + 12 + 4 * i, 1), :] * weight)
        square = points[0] * points[0] + points[1] * points[1] + points[2] * points[2]
        for i in range(3):
            slab[i : i + 1, :] = -2.0 * points[i]
        slab[3:4, :] = square
        first, second, third = split_three(slab[...])
        right = jnp.concatenate([first, second, first, second, third, first]).astype(jnp.bfloat16)
        left = lifted[target, 0:T_ROWS, 0:48]
        square = square + 2.0 * delta2
        along = points[0] * forces[0] + points[1] * forces[1] + points[2] * forces[2]
        for i in range(3):
            columns[i : i + 1, :] = forces[i]
            for j in range(3):
                columns[3 + 3 * i + j : 4 + 3 * i + j, :] = forces[i] * points[j]
            columns[12 + i : 13 + i, :] = square * forces[i] + along * points[i]
        wide = columns[...]
        wide_high = wide.astype(jnp.bfloat16)
        wide_low = (wide - wide_high.astype(jnp.float32)).astype(jnp.bfloat16)
        both = jnp.concatenate([wide_high, wide_low], axis=0)
        parts, wides = [], []
        for step in range(S_PAD // CHUNK):
            span = slice(step * CHUNK, (step + 1) * CHUNK)
            softened = jnp.dot(left, right[:, span], preferred_element_type=jnp.float32)
            inverse = lax.rsqrt(softened)
            cube = inverse * inverse * inverse
            cube_high = cube.astype(jnp.bfloat16)
            cube_low = (cube - cube_high.astype(jnp.float32)).astype(jnp.bfloat16)
            parts += [cube_high, cube_low]
            wides += [both[:, span], both[:, span]]
        part = jnp.concatenate(parts, axis=1)
        wide = jnp.concatenate(wides, axis=1)
        total = lax.dot_general(part, wide, NT, preferred_element_type=jnp.float32)
        totals[target, 0:T_ROWS, 0 : 2 * COLS] += total

    @pl.loop(0, filled // 2)
    def _(item):
        process(2 * item, columns.at[0], slab.at[0])
        process(2 * item + 1, columns.at[1], slab.at[1])

    @pl.when(filled % 2 == 1)
    def _():
        process(filled - 1, columns.at[0], slab.at[0])

    for vesicle in range(4):
        turned = jnp.transpose(totals[vesicle])
        sums = turned[0:COLS] + turned[COLS : 2 * COLS]
        x = [row_points[4 * i + vesicle : 4 * i + vesicle + 1, :] for i in range(3)]
        plain = [sums[i : i + 1, :] for i in range(3)]
        cross = [[sums[3 + 3 * i + j : 4 + 3 * i + j, :] for j in range(3)] for i in range(3)]
        last = [sums[12 + i : 13 + i, :] for i in range(3)]
        square = x[0] * x[0] + x[1] * x[1] + x[2] * x[2]
        along = x[0] * plain[0] + x[1] * plain[1] + x[2] * plain[2]
        trace = cross[0][0] + cross[1][1] + cross[2][2]
        for i in range(3):
            value = square * plain[i] + x[i] * (along - trace) + last[i]
            for j in range(3):
                value = value - x[j] * (2.0 * cross[i][j] + cross[j][i])
            columns[0, 4 * i + vesicle : 4 * i + vesicle + 1, 0:T_PAD] = value * (0.125 / math.pi)
    result = jnp.dot(
        columns[0, :, 0:T_PAD],
        analysis_ref[0:T_PAD, :],
        precision=lax.Precision.HIGHEST,
        preferred_element_type=jnp.float32,
    )
    for i in range(3):
        out_ref[i] = result[4 * i : 4 * i + 4, 0 : HEAD + TAIL]


def near(names, packed, tables):
    vmem = pl.BlockSpec(memory_space=pltpu.VMEM)
    return pl.pallas_call(
        near_kernel,
        out_shape=jax.ShapeDtypeStruct((3, 4, HEAD + TAIL), jnp.float32),
        in_specs=[pl.BlockSpec(memory_space=pltpu.SMEM)] + [pl.BlockSpec(memory_space=pl.ANY)] * 2 + [vmem] * 2,
        out_specs=vmem,
        scratch_shapes=[
            pltpu.VMEM((27, 24, 512), jnp.float32),
            pltpu.VMEM((27 * 24, S_PAD), jnp.float32),
            pltpu.VMEM((27, 24, HEAD), jnp.float32),
            pltpu.VMEM((4, T_PAD, HEAD), jnp.bfloat16),
            pltpu.VMEM((2, 8, S_PAD), jnp.float32),
            pltpu.VMEM((4, T_PAD, HEAD), jnp.float32),
            pltpu.VMEM((2, COLS, S_PAD), jnp.float32),
            pltpu.SMEM((360,), jnp.int32),
            pltpu.SMEM((360,), jnp.int32),
            pltpu.VMEM((27, MESSAGE, HEAD), jnp.float32),
            pltpu.VMEM((512, S_PAD), jnp.bfloat16),
            pltpu.SemaphoreType.DMA((2,)),
        ],
        compiler_params=pltpu.CompilerParams(vmem_limit_bytes=48 * 1024 * 1024),
        name="near",
    )(names, packed, *tables)


def on_device(sizes, shape_coef, density_coef, pair_count, pair_slots):
    shape, density = (
        jnp.swapaxes(part[0, 0, 0], 0, 1) for part in (shape_coef, density_coef)
    )
    slots = pair_slots[0, 0, 0].T
    packed, names = halo(shape, density, slots, pair_count.reshape(1, 1), sizes)
    result = near(names, packed, grid_tables())
    return jnp.swapaxes(result, 0, 1)[None, None, None]


def solution(mesh):
    placed = (
        P("gx", "gy", "gz", None, None, None),
        P("gx", "gy", "gz", None, None, None),
        P("gx", "gy", "gz"),
        P("gx", "gy", "gz", None, None),
    )
    return jax.shard_map(
        functools.partial(on_device, tuple(mesh.shape[axis] for axis in AXES)),
        mesh=mesh,
        in_specs=placed,
        out_specs=P("gx", "gy", "gz", None, None, None),
        check_vma=False,
    )
```

```python
import functools
import itertools
import math

import jax
import jax.numpy as jnp
import numpy as np
from jax import lax
from jax.experimental import pallas as pl
from jax.experimental.pallas import tpu as pltpu
from jax.sharding import PartitionSpec as P

P_SIZE = 12
Q = 24


blob_radius = 0.25

def gauss_nodes(node_count):
    numbers = np.arange(1, node_count + 1)
    cosine = np.cos(np.pi * (numbers - 0.25) / (node_count + 0.5))

    def legendre_pair(points):
        legendre_prev = np.ones(points.shape)
        legendre_next = np.array(points)
        for degree in range(2, node_count + 1):
            legendre_prev, legendre_next = (
                legendre_next,
                ((2.0 * degree - 1.0) * points * legendre_next - (degree - 1.0) * legendre_prev)
                / degree,
            )
        slope = node_count * (points * legendre_next - legendre_prev) / (points * points - 1.0)
        return (legendre_next, slope)

    for newton_step in range(100):
        value_now, slope = legendre_pair(cosine)
        cosine = cosine - value_now / slope
    value_now, slope = legendre_pair(cosine)
    weights = 2.0 / ((1.0 - cosine * cosine) * slope * slope)
    return (np.array(cosine[::-1]), np.array(weights[::-1]))


def harmonic_table(top_degree, latitudes, longitudes):
    cosine, gauss_weight = gauss_nodes(latitudes)
    sine_theta = np.sqrt(1.0 - cosine * cosine)
    angles = 2.0 * np.pi * np.arange(longitudes) / longitudes
    legendre = np.zeros((top_degree + 1, top_degree + 1, latitudes))
    legendre[0, 0] = np.sqrt(0.25 / np.pi)
    for degree_m in range(1, top_degree + 1):
        legendre[degree_m, degree_m] = (
            np.sqrt((2.0 * degree_m + 1.0) / (2.0 * degree_m))
            * sine_theta
            * legendre[degree_m - 1, degree_m - 1]
        )
    for degree_m in range(top_degree + 1):
        if degree_m + 1 <= top_degree:
            legendre[degree_m + 1, degree_m] = (
                np.sqrt(2.0 * degree_m + 3.0) * cosine * legendre[degree_m, degree_m]
            )
        for degree_l in range(degree_m + 2, top_degree + 1):
            factor = np.sqrt(
                (4.0 * degree_l * degree_l - 1.0) / (degree_l * degree_l - degree_m * degree_m)
            )
            lagged = np.sqrt(
                ((degree_l - 1.0) * (degree_l - 1.0) - degree_m * degree_m)
                / (4.0 * (degree_l - 1.0) * (degree_l - 1.0) - 1.0)
            )
            legendre[degree_l, degree_m] = factor * (
                cosine * legendre[degree_l - 1, degree_m]
                - lagged * legendre[degree_l - 2, degree_m]
            )
    table_rows = []
    for degree_l in range(top_degree + 1):
        for signed in range(-degree_l, degree_l + 1):
            polar_part = legendre[degree_l, abs(signed)][:, None]
            if signed > 0:
                azimuth = np.sqrt(2.0) * np.cos(signed * angles)
            elif signed < 0:
                azimuth = np.sqrt(2.0) * np.sin(-signed * angles)
            else:
                azimuth = np.ones(longitudes)
            table_rows.append((polar_part * azimuth[None, :]).reshape(-1))
    synthesis = np.stack(table_rows)
    weights = np.repeat(gauss_weight, longitudes) * (2.0 * np.pi / longitudes)
    return (synthesis, weights)

AXES = ("gx", "gy", "gz")
OFFSETS = list(itertools.product((-1, 0, 1), repeat=3))
HEAD = 128
TAIL = 41
MESSAGE = 40
T_PAD = 384
T_ROWS = 352
S_PAD = 1280
CHUNK = 1280
COLS = 16


def split_table(table):
    high = table.astype(np.float32).astype(jnp.bfloat16)
    low = (table - high.astype(np.float64)).astype(jnp.bfloat16)
    pad = np.zeros((512 - 3 * table.shape[0], table.shape[1]), jnp.bfloat16)
    return np.concatenate(
        [high[:HEAD], low[:HEAD], high[:HEAD], high[HEAD:], low[HEAD:], high[HEAD:], pad]
    )


def grid_tables():
    target_synth, target_weight = harmonic_table(P_SIZE, P_SIZE + 1, 2 * (P_SIZE + 1))
    upsample_synth, upsample_weight = harmonic_table(P_SIZE, Q + 1, 2 * (Q + 1))
    targets, sources = target_synth.shape[1], upsample_synth.shape[1]
    target_wide = np.pad(target_synth, ((0, 0), (0, T_PAD - targets)))
    source_wide = np.pad(upsample_synth, ((0, 0), (0, S_PAD - sources)))
    weight_rows = np.pad(upsample_weight, (0, S_PAD - sources)).reshape(-1, 256)
    weight_rows = np.pad(weight_rows, ((0, 8 - weight_rows.shape[0]), (0, 0)))
    analysis = np.pad(
        (target_synth * target_weight[None, :]).T,
        ((0, T_PAD - targets), (0, 256 - target_synth.shape[0])),
    )
    return (
        jnp.asarray(split_table(source_wide)),
        jnp.asarray(np.ascontiguousarray(split_table(target_wide).T)),
        jnp.asarray(np.concatenate([analysis, weight_rows]), dtype=jnp.float32),
    )


def halo_kernel(
    sizes, shape_hbm, density_hbm, slots_hbm, count_hbm, out_ref,
    own_ref, tail_ref, blank_ref, shape_ref, density_ref, slots_ref, count_ref,
    send_sem, recv_sem, local_sem,
):
    loads = [
        pltpu.make_async_copy(source, target, local_sem.at[27 + i])
        for i, (source, target) in enumerate(
            (
                (shape_hbm, shape_ref),
                (density_hbm, density_ref),
                (slots_hbm, slots_ref),
                (count_hbm, count_ref),
            )
        )
    ]
    for load in loads:
        load.start()
    here = [lax.axis_index(axis) for axis in AXES]

    def place(offset):
        there = [h + o for h, o in zip(here, offset)]
        exists = None
        for spot, o, size in zip(there, offset, sizes):
            if o:
                inside = (spot >= 0) & (spot < size)
                exists = inside if exists is None else exists & inside
        return tuple(there), exists

    barrier = pltpu.get_barrier_semaphore()
    around = 1
    for h, size in zip(here, sizes):
        around = around * (1 + (h > 0).astype(jnp.int32) + (h < size - 1).astype(jnp.int32))
    for offset in OFFSETS:
        if any(offset):
            there, exists = place(offset)

            @pl.when(exists)
            def _():
                pl.semaphore_signal(
                    barrier, inc=1, device_id=there, device_id_type=pl.DeviceIdType.MESH
                )

    blank_ref[...] = jnp.zeros(blank_ref.shape, jnp.float32)
    own_ref[32:MESSAGE, :] = jnp.zeros((MESSAGE - 32, HEAD), jnp.float32)
    tail_ref[...] = jnp.zeros(tail_ref.shape, jnp.float32)
    for load in loads:
        load.wait()
    for start, source in ((0, shape_ref), (12, density_ref)):
        for i in range(3):
            rows = slice(start + 4 * i, start + 4 * i + 4)
            own_ref[rows, :] = source[i, :, 0:HEAD]
            tail_ref[rows, 0:TAIL] = source[i, :, HEAD : HEAD + TAIL]
    own_ref[24:32, :] = (
        tail_ref[0:8, :]
        + pltpu.roll(tail_ref[8:16, :], TAIL, 1)
        + pltpu.roll(tail_ref[16:24, :], 2 * TAIL, 1)
    )
    for i in range(2):
        own_ref[32 + i : 33 + i, 0:12] = slots_ref[i : i + 1, :].astype(jnp.float32)
    own_ref[34:35, :] = jnp.full((1, HEAD), count_ref[0, 0].astype(jnp.float32))
    pl.semaphore_wait(barrier, around - 1)

    def transfer(code):
        there, exists = place(OFFSETS[code])
        copy = pltpu.make_async_remote_copy(
            src_ref=own_ref,
            dst_ref=out_ref.at[26 - code],
            send_sem=send_sem.at[code],
            recv_sem=recv_sem.at[26 - code],
            device_id=there,
            device_id_type=pl.DeviceIdType.MESH,
        )
        return copy, exists

    for code in range(27):
        if code != 13:
            copy, exists = transfer(code)

            @pl.when(exists)
            def _():
                copy.start()

    def fill(code):
        source = own_ref if code == 13 else blank_ref
        return pltpu.make_async_copy(source, out_ref.at[code], local_sem.at[code])

    fill(13).start()
    for code in range(27):
        if code != 13:
            there, exists = place(OFFSETS[code])

            @pl.when(jnp.logical_not(exists))
            def _():
                fill(code).start()

    fill(13).wait()
    for code in range(27):
        if code != 13:
            there, exists = place(OFFSETS[code])

            @pl.when(jnp.logical_not(exists))
            def _():
                fill(code).wait()

    for code in range(27):
        if code != 13:
            there, exists = place(OFFSETS[code])

            @pl.when(exists)
            def _():
                copy = pltpu.make_async_remote_copy(
                    src_ref=own_ref,
                    dst_ref=out_ref.at[code],
                    send_sem=send_sem.at[code],
                    recv_sem=recv_sem.at[code],
                    device_id=there,
                    device_id_type=pl.DeviceIdType.MESH,
                )
                copy.wait()


def halo(shape, density, slots, count, sizes):
    hbm = pl.BlockSpec(memory_space=pltpu.HBM)
    return pl.pallas_call(
        functools.partial(halo_kernel, sizes),
        out_shape=jax.ShapeDtypeStruct((27, MESSAGE, HEAD), jnp.float32),
        in_specs=[hbm] * 4,
        out_specs=hbm,
        scratch_shapes=[
            pltpu.VMEM((MESSAGE, HEAD), jnp.float32),
            pltpu.VMEM((24, HEAD), jnp.float32),
            pltpu.VMEM((MESSAGE, HEAD), jnp.float32),
            pltpu.VMEM(shape.shape, jnp.float32),
            pltpu.VMEM(density.shape, jnp.float32),
            pltpu.VMEM(slots.shape, jnp.int32),
            pltpu.SMEM(count.shape, jnp.int32),
            pltpu.SemaphoreType.DMA((27,)),
            pltpu.SemaphoreType.DMA((27,)),
            pltpu.SemaphoreType.DMA((31,)),
        ],
        compiler_params=pltpu.CompilerParams(collective_id=0, has_side_effects=True),
        name="halo",
    )(shape, density, slots, count)


NT = (((1,), (1,)), ((), ()))


def split_three(value):
    first = value.astype(jnp.bfloat16).astype(jnp.float32)
    rest = value - first
    second = rest.astype(jnp.bfloat16).astype(jnp.float32)
    return first, second, rest - second


def near_kernel(
    packed_hbm, source_hbm, target_hbm, analysis_hbm, out_ref,
    coef, grids, centre, lifted, slab, totals, columns, target_list, source_list,
    packed_ref, source_table, target_table, analysis_ref, flat_ref, names_ref, copy_sem,
):
    delta2 = blob_radius * blob_radius
    loads = [
        pltpu.make_async_copy(source, target, copy_sem.at[i])
        for i, (source, target) in enumerate(
            (
                (packed_hbm, packed_ref),
                (target_hbm, target_table),
                (source_hbm, source_table),
                (analysis_hbm, analysis_ref),
            )
        )
    ]
    for load in loads:
        load.start()
    loads[0].wait()
    lane = lax.broadcasted_iota(jnp.int32, (1, HEAD), 1)
    for code in range(27):
        flat = packed_ref[code, 32:MESSAGE, :].astype(jnp.int32)
        flat_ref[code : code + 1, :] = jnp.where(
            lane < 12, flat[0:1], jnp.where(lane < 24, pltpu.roll(flat, 12, 1)[1:2], flat[2:3])
        )
    names_copy = pltpu.make_async_copy(flat_ref, names_ref, copy_sem.at[4])
    names_copy.start()
    lanes = lax.broadcasted_iota(jnp.int32, (27, 8, HEAD), 2)
    rows8 = lax.broadcasted_iota(jnp.int32, (27, 8, HEAD), 1)
    tails = packed_ref[:, 24:32, :]
    for group in range(3):
        head = packed_ref[:, 8 * group : 8 * group + 8, :]
        centre[:, 8 * group : 8 * group + 8, :] = jnp.broadcast_to(
            head[:, :, 0:1] * (0.5 / math.sqrt(math.pi)), head.shape
        )
        head = jnp.where((lanes == 0) & (rows8 + 8 * group < 12), 0.0, head)
        head_high = head.astype(jnp.bfloat16).astype(jnp.float32)
        tail = tails if group == 0 else pltpu.roll(tails, HEAD - TAIL * group, 2)
        tail = jnp.where(lanes < TAIL, tail, 0.0)
        tail_high = tail.astype(jnp.bfloat16).astype(jnp.float32)
        tail_low = tail - tail_high
        rows = slice(8 * group, 8 * group + 8)
        coef[:, rows, 0:128] = head_high
        coef[:, rows, 128:256] = head_high
        coef[:, rows, 256:384] = head - head_high
        coef[:, rows, 384:512] = (
            tail_high + pltpu.roll(tail_high, TAIL, 2) + pltpu.roll(tail_low, 2 * TAIL, 2)
        )

    own = coef[13].astype(jnp.bfloat16)
    loads[1].wait()
    row_points = lax.dot_general(own, target_table[...], NT, preferred_element_type=jnp.float32)

    slab[...] = jnp.zeros(slab.shape, jnp.float32)
    ones = jnp.ones((1, T_PAD), jnp.float32)
    for vesicle in range(4):
        x = [row_points[4 * i + vesicle : 4 * i + vesicle + 1, :] for i in range(3)]
        for i in range(3):
            slab[0, i : i + 1, 0:T_PAD] = x[i]
        slab[0, 3:4, 0:T_PAD] = ones
        slab[0, 4:5, 0:T_PAD] = x[0] * x[0] + x[1] * x[1] + x[2] * x[2] + delta2
        first, second, third = split_three(slab[0, :, 0:T_PAD])
        lifted[vesicle] = jnp.transpose(
            jnp.concatenate(
                [first, first, second, second, first, third]
                + [jnp.zeros((HEAD - 48, T_PAD), jnp.float32)]
            )
        ).astype(jnp.bfloat16)
    for copy in range(2):
        slab[copy, 4:5, :] = jnp.ones((1, S_PAD), jnp.float32)

    loads[2].wait()
    everything = coef[...].reshape(27 * 24, 512).astype(jnp.bfloat16)

    @pl.loop(0, S_PAD // CHUNK)
    def _(step):
        span = pl.ds(pl.multiple_of(step * CHUNK, CHUNK), CHUNK)
        grids[:, span] = jnp.dot(
            everything, source_table[:, span], preferred_element_type=jnp.float32
        )

    names_copy.wait()
    def scan_device(code, filled):
        def scan_slot(slot, filled):
            first = names_ref[code, slot]
            second = names_ref[code, 12 + slot]
            target_list[filled] = second & 3
            source_list[filled] = code * 4 + (first & 3)
            return filled + ((second >> 2) == 26 - code).astype(jnp.int32)

        return lax.fori_loop(0, names_ref[code, 24], scan_slot, filled)

    def own_slot(slot, filled):
        target_list[filled] = names_ref[13, slot] & 3
        source_list[filled] = names_ref[13, 12 + slot]
        return filled + 1

    filled = lax.fori_loop(0, 27, scan_device, 0)
    filled = lax.fori_loop(0, names_ref[13, 24], own_slot, filled)

    loads[3].wait()
    weight = jnp.concatenate(
        [analysis_ref[T_PAD + i : T_PAD + i + 1, :] for i in range(S_PAD // 256)], axis=1
    )
    totals[...] = jnp.zeros(totals.shape, jnp.float32)

    def process(item, columns, slab):
        target = target_list[item]
        entry = source_list[item]
        device = entry >> 2
        vesicle = entry & 3
        base = device * 24 + vesicle
        points, forces = [], []
        for i in range(3):
            moved = centre[device, pl.ds(4 * i + vesicle, 1), :] - centre[13, pl.ds(4 * i + target, 1), :]
            points.append(grids[pl.ds(base + 4 * i, 1), :] + jnp.concatenate([moved] * (S_PAD // HEAD), axis=1))
            forces.append(grids[pl.ds(base + 12 + 4 * i, 1), :] * weight)
        square = points[0] * points[0] + points[1] * points[1] + points[2] * points[2]
        for i in range(3):
            slab[i : i + 1, :] = -2.0 * points[i]
        slab[3:4, :] = square
        first, second, third = split_three(slab[...])
        right = jnp.concatenate([first, second, first, second, third, first]).astype(jnp.bfloat16)
        left = lifted[target, 0:T_ROWS, 0:48]
        square = square + 2.0 * delta2
        along = points[0] * forces[0] + points[1] * forces[1] + points[2] * forces[2]
        for i in range(3):
            columns[i : i + 1, :] = forces[i]
            for j in range(3):
                columns[3 + 3 * i + j : 4 + 3 * i + j, :] = forces[i] * points[j]
            columns[12 + i : 13 + i, :] = square * forces[i] + along * points[i]
        wide = columns[...]
        wide_high = wide.astype(jnp.bfloat16)
        wide_low = (wide - wide_high.astype(jnp.float32)).astype(jnp.bfloat16)
        both = jnp.concatenate([wide_high, wide_low], axis=0)
        parts, wides = [], []
        for step in range(S_PAD // CHUNK):
            span = slice(step * CHUNK, (step + 1) * CHUNK)
            softened = jnp.dot(left, right[:, span], preferred_element_type=jnp.float32)
            inverse = lax.rsqrt(softened)
            cube = inverse * inverse * inverse
            cube_high = cube.astype(jnp.bfloat16)
            cube_low = (cube - cube_high.astype(jnp.float32)).astype(jnp.bfloat16)
            parts += [cube_high, cube_low]
            wides += [both[:, span], both[:, span]]
        part = jnp.concatenate(parts, axis=1)
        wide = jnp.concatenate(wides, axis=1)
        total = lax.dot_general(part, wide, NT, preferred_element_type=jnp.float32)
        totals[target, 0:T_ROWS, 0 : 2 * COLS] += total

    @pl.loop(0, filled // 2)
    def _(item):
        process(2 * item, columns.at[0], slab.at[0])
        process(2 * item + 1, columns.at[1], slab.at[1])

    @pl.when(filled % 2 == 1)
    def _():
        process(filled - 1, columns.at[0], slab.at[0])

    for vesicle in range(4):
        turned = jnp.transpose(totals[vesicle])
        sums = turned[0:COLS] + turned[COLS : 2 * COLS]
        x = [row_points[4 * i + vesicle : 4 * i + vesicle + 1, :] for i in range(3)]
        plain = [sums[i : i + 1, :] for i in range(3)]
        cross = [[sums[3 + 3 * i + j : 4 + 3 * i + j, :] for j in range(3)] for i in range(3)]
        last = [sums[12 + i : 13 + i, :] for i in range(3)]
        square = x[0] * x[0] + x[1] * x[1] + x[2] * x[2]
        along = x[0] * plain[0] + x[1] * plain[1] + x[2] * plain[2]
        trace = cross[0][0] + cross[1][1] + cross[2][2]
        for i in range(3):
            value = square * plain[i] + x[i] * (along - trace) + last[i]
            for j in range(3):
                value = value - x[j] * (2.0 * cross[i][j] + cross[j][i])
            columns[0, 4 * i + vesicle : 4 * i + vesicle + 1, 0:T_PAD] = value * (0.125 / math.pi)
    result = jnp.dot(
        columns[0, :, 0:T_PAD],
        analysis_ref[0:T_PAD, :],
        precision=lax.Precision.HIGHEST,
        preferred_element_type=jnp.float32,
    )
    for i in range(3):
        out_ref[i] = result[4 * i : 4 * i + 4, 0 : HEAD + TAIL]


def near(packed, tables):
    vmem = pl.BlockSpec(memory_space=pltpu.VMEM)
    return pl.pallas_call(
        near_kernel,
        out_shape=jax.ShapeDtypeStruct((3, 4, HEAD + TAIL), jnp.float32),
        in_specs=[pl.BlockSpec(memory_space=pltpu.HBM)] * 4,
        out_specs=vmem,
        scratch_shapes=[
            pltpu.VMEM((27, 24, 512), jnp.float32),
            pltpu.VMEM((27 * 24, S_PAD), jnp.float32),
            pltpu.VMEM((27, 24, HEAD), jnp.float32),
            pltpu.VMEM((4, T_PAD, HEAD), jnp.bfloat16),
            pltpu.VMEM((2, 8, S_PAD), jnp.float32),
            pltpu.VMEM((4, T_PAD, HEAD), jnp.float32),
            pltpu.VMEM((2, COLS, S_PAD), jnp.float32),
            pltpu.SMEM((360,), jnp.int32),
            pltpu.SMEM((360,), jnp.int32),
            pltpu.VMEM((27, MESSAGE, HEAD), jnp.float32),
            pltpu.VMEM((512, S_PAD), jnp.bfloat16),
            pltpu.VMEM((T_PAD, 512), jnp.bfloat16),
            pltpu.VMEM((T_PAD + 8, 256), jnp.float32),
            pltpu.VMEM((32, HEAD), jnp.int32),
            pltpu.SMEM((32, HEAD), jnp.int32),
            pltpu.SemaphoreType.DMA((5,)),
        ],
        compiler_params=pltpu.CompilerParams(vmem_limit_bytes=64 * 1024 * 1024),
        name="near",
    )(packed, *tables)


def on_device(sizes, shape_coef, density_coef, pair_count, pair_slots):
    shape, density = (
        jnp.swapaxes(part[0, 0, 0], 0, 1) for part in (shape_coef, density_coef)
    )
    slots = pair_slots[0, 0, 0].T
    packed = halo(shape, density, slots, pair_count.reshape(1, 1), sizes)
    result = near(packed, grid_tables())
    return jnp.swapaxes(result, 0, 1)[None, None, None]


def solution(mesh):
    placed = (
        P("gx", "gy", "gz", None, None, None),
        P("gx", "gy", "gz", None, None, None),
        P("gx", "gy", "gz"),
        P("gx", "gy", "gz", None, None),
    )
    return jax.shard_map(
        functools.partial(on_device, tuple(mesh.shape[axis] for axis in AXES)),
        mesh=mesh,
        in_specs=placed,
        out_specs=P("gx", "gy", "gz", None, None, None),
        check_vma=False,
    )
```

```python
import functools
import itertools
import math

import jax
import jax.numpy as jnp
import numpy as np
from jax import lax
from jax.experimental import pallas as pl
from jax.experimental.pallas import tpu as pltpu
from jax.sharding import PartitionSpec as P

P_SIZE = 12
Q = 24


blob_radius = 0.25

def gauss_nodes(node_count):
    numbers = np.arange(1, node_count + 1)
    cosine = np.cos(np.pi * (numbers - 0.25) / (node_count + 0.5))

    def legendre_pair(points):
        legendre_prev = np.ones(points.shape)
        legendre_next = np.array(points)
        for degree in range(2, node_count + 1):
            legendre_prev, legendre_next = (
                legendre_next,
                ((2.0 * degree - 1.0) * points * legendre_next - (degree - 1.0) * legendre_prev)
                / degree,
            )
        slope = node_count * (points * legendre_next - legendre_prev) / (points * points - 1.0)
        return (legendre_next, slope)

    for newton_step in range(100):
        value_now, slope = legendre_pair(cosine)
        cosine = cosine - value_now / slope
    value_now, slope = legendre_pair(cosine)
    weights = 2.0 / ((1.0 - cosine * cosine) * slope * slope)
    return (np.array(cosine[::-1]), np.array(weights[::-1]))


def harmonic_table(top_degree, latitudes, longitudes):
    cosine, gauss_weight = gauss_nodes(latitudes)
    sine_theta = np.sqrt(1.0 - cosine * cosine)
    angles = 2.0 * np.pi * np.arange(longitudes) / longitudes
    legendre = np.zeros((top_degree + 1, top_degree + 1, latitudes))
    legendre[0, 0] = np.sqrt(0.25 / np.pi)
    for degree_m in range(1, top_degree + 1):
        legendre[degree_m, degree_m] = (
            np.sqrt((2.0 * degree_m + 1.0) / (2.0 * degree_m))
            * sine_theta
            * legendre[degree_m - 1, degree_m - 1]
        )
    for degree_m in range(top_degree + 1):
        if degree_m + 1 <= top_degree:
            legendre[degree_m + 1, degree_m] = (
                np.sqrt(2.0 * degree_m + 3.0) * cosine * legendre[degree_m, degree_m]
            )
        for degree_l in range(degree_m + 2, top_degree + 1):
            factor = np.sqrt(
                (4.0 * degree_l * degree_l - 1.0) / (degree_l * degree_l - degree_m * degree_m)
            )
            lagged = np.sqrt(
                ((degree_l - 1.0) * (degree_l - 1.0) - degree_m * degree_m)
                / (4.0 * (degree_l - 1.0) * (degree_l - 1.0) - 1.0)
            )
            legendre[degree_l, degree_m] = factor * (
                cosine * legendre[degree_l - 1, degree_m]
                - lagged * legendre[degree_l - 2, degree_m]
            )
    table_rows = []
    for degree_l in range(top_degree + 1):
        for signed in range(-degree_l, degree_l + 1):
            polar_part = legendre[degree_l, abs(signed)][:, None]
            if signed > 0:
                azimuth = np.sqrt(2.0) * np.cos(signed * angles)
            elif signed < 0:
                azimuth = np.sqrt(2.0) * np.sin(-signed * angles)
            else:
                azimuth = np.ones(longitudes)
            table_rows.append((polar_part * azimuth[None, :]).reshape(-1))
    synthesis = np.stack(table_rows)
    weights = np.repeat(gauss_weight, longitudes) * (2.0 * np.pi / longitudes)
    return (synthesis, weights)

AXES = ("gx", "gy", "gz")
OFFSETS = list(itertools.product((-1, 0, 1), repeat=3))
HEAD = 128
TAIL = 41
MESSAGE = 40
T_PAD = 384
T_ROWS = 352
S_PAD = 1280
CHUNK = 1280
UNROLL = 4
COLS = 16


def split_table(table):
    high = table.astype(np.float32).astype(jnp.bfloat16)
    low = (table - high.astype(np.float64)).astype(jnp.bfloat16)
    pad = np.zeros((512 - 3 * table.shape[0], table.shape[1]), jnp.bfloat16)
    return np.concatenate(
        [high[:HEAD], low[:HEAD], high[:HEAD], high[HEAD:], low[HEAD:], high[HEAD:], pad]
    )


def grid_tables():
    target_synth, target_weight = harmonic_table(P_SIZE, P_SIZE + 1, 2 * (P_SIZE + 1))
    upsample_synth, upsample_weight = harmonic_table(P_SIZE, Q + 1, 2 * (Q + 1))
    targets, sources = target_synth.shape[1], upsample_synth.shape[1]
    target_wide = np.pad(target_synth, ((0, 0), (0, T_PAD - targets)))
    source_wide = np.pad(upsample_synth, ((0, 0), (0, S_PAD - sources)))
    weight_rows = np.pad(upsample_weight, (0, S_PAD - sources)).reshape(-1, 256)
    weight_rows = np.pad(weight_rows, ((0, 8 - weight_rows.shape[0]), (0, 0)))
    analysis = np.pad(
        (target_synth * target_weight[None, :]).T,
        ((0, T_PAD - targets), (0, 256 - target_synth.shape[0])),
    )
    return (
        jnp.asarray(split_table(source_wide)),
        jnp.asarray(np.ascontiguousarray(split_table(target_wide).T)),
        jnp.asarray(np.concatenate([analysis, weight_rows]), dtype=jnp.float32),
    )


def halo_kernel(
    sizes, shape_hbm, density_hbm, slots_hbm, count_hbm, out_ref,
    own_ref, tail_ref, blank_ref, shape_ref, density_ref, slots_ref, count_ref,
    send_sem, recv_sem, local_sem,
):
    loads = [
        pltpu.make_async_copy(source, target, local_sem.at[27 + i])
        for i, (source, target) in enumerate(
            (
                (shape_hbm, shape_ref),
                (density_hbm, density_ref),
                (slots_hbm, slots_ref),
                (count_hbm, count_ref),
            )
        )
    ]
    for load in loads:
        load.start()
    here = [lax.axis_index(axis) for axis in AXES]

    def place(offset):
        there = [h + o for h, o in zip(here, offset)]
        exists = None
        for spot, o, size in zip(there, offset, sizes):
            if o:
                inside = (spot >= 0) & (spot < size)
                exists = inside if exists is None else exists & inside
        return tuple(there), exists

    barrier = pltpu.get_barrier_semaphore()
    around = 1
    for h, size in zip(here, sizes):
        around = around * (1 + (h > 0).astype(jnp.int32) + (h < size - 1).astype(jnp.int32))
    for offset in OFFSETS:
        if any(offset):
            there, exists = place(offset)

            @pl.when(exists)
            def _():
                pl.semaphore_signal(
                    barrier, inc=1, device_id=there, device_id_type=pl.DeviceIdType.MESH
                )

    blank_ref[...] = jnp.zeros(blank_ref.shape, jnp.float32)
    tail_ref[...] = jnp.zeros(tail_ref.shape, jnp.float32)
    for load in loads:
        load.wait()
    for start, source in ((0, shape_ref), (12, density_ref)):
        for i in range(3):
            rows = slice(start + 4 * i, start + 4 * i + 4)
            own_ref[rows, :] = source[i, :, 0:HEAD]
            tail_ref[rows, 0:TAIL] = source[i, :, HEAD : HEAD + TAIL]
    own_ref[24:32, :] = (
        tail_ref[0:8, :]
        + pltpu.roll(tail_ref[8:16, :], TAIL, 1)
        + pltpu.roll(tail_ref[16:24, :], 2 * TAIL, 1)
    )
    names = jnp.full((1, HEAD), count_ref[0, 0].astype(jnp.float32))
    own_ref[32:MESSAGE, :] = jnp.broadcast_to(names, (MESSAGE - 32, HEAD))
    for i in range(2):
        own_ref[32:33, 12 * i : 12 * i + 12] = slots_ref[i : i + 1, :].astype(jnp.float32)
    pl.semaphore_wait(barrier, around - 1)

    def transfer(code):
        there, exists = place(OFFSETS[code])
        copy = pltpu.make_async_remote_copy(
            src_ref=own_ref,
            dst_ref=out_ref.at[26 - code],
            send_sem=send_sem.at[code],
            recv_sem=recv_sem.at[26 - code],
            device_id=there,
            device_id_type=pl.DeviceIdType.MESH,
        )
        return copy, exists

    for code in range(27):
        if code != 13:
            copy, exists = transfer(code)

            @pl.when(exists)
            def _():
                copy.start()

    def fill(code):
        source = own_ref if code == 13 else blank_ref
        return pltpu.make_async_copy(source, out_ref.at[code], local_sem.at[code])

    fill(13).start()
    for code in range(27):
        if code != 13:
            there, exists = place(OFFSETS[code])

            @pl.when(jnp.logical_not(exists))
            def _():
                fill(code).start()

    fill(13).wait()
    for code in range(27):
        if code != 13:
            there, exists = place(OFFSETS[code])

            @pl.when(jnp.logical_not(exists))
            def _():
                fill(code).wait()

    for code in range(27):
        if code != 13:
            there, exists = place(OFFSETS[code])

            @pl.when(exists)
            def _():
                copy = pltpu.make_async_remote_copy(
                    src_ref=own_ref,
                    dst_ref=out_ref.at[code],
                    send_sem=send_sem.at[code],
                    recv_sem=recv_sem.at[code],
                    device_id=there,
                    device_id_type=pl.DeviceIdType.MESH,
                )
                copy.wait()


def halo(shape, density, slots, count, sizes):
    hbm = pl.BlockSpec(memory_space=pltpu.HBM)
    return pl.pallas_call(
        functools.partial(halo_kernel, sizes),
        out_shape=jax.ShapeDtypeStruct((27, MESSAGE, HEAD), jnp.float32),
        in_specs=[hbm] * 4,
        out_specs=hbm,
        scratch_shapes=[
            pltpu.VMEM((MESSAGE, HEAD), jnp.float32),
            pltpu.VMEM((24, HEAD), jnp.float32),
            pltpu.VMEM((MESSAGE, HEAD), jnp.float32),
            pltpu.VMEM(shape.shape, jnp.float32),
            pltpu.VMEM(density.shape, jnp.float32),
            pltpu.VMEM(slots.shape, jnp.int32),
            pltpu.SMEM(count.shape, jnp.int32),
            pltpu.SemaphoreType.DMA((27,)),
            pltpu.SemaphoreType.DMA((27,)),
            pltpu.SemaphoreType.DMA((31,)),
        ],
        compiler_params=pltpu.CompilerParams(collective_id=0, has_side_effects=True),
        name="halo",
    )(shape, density, slots, count)


NT = (((1,), (1,)), ((), ()))


def split_three(value):
    first = value.astype(jnp.bfloat16).astype(jnp.float32)
    rest = value - first
    second = rest.astype(jnp.bfloat16).astype(jnp.float32)
    return first, second, rest - second


def near_kernel(
    packed_hbm, source_hbm, target_hbm, analysis_hbm, out_ref,
    coef, grids, centre, lifted, slab, totals, columns, target_list, source_list,
    packed_ref, source_table, target_table, analysis_ref, flat_ref, names_ref, copy_sem,
):
    delta2 = blob_radius * blob_radius
    loads = [
        pltpu.make_async_copy(source, target, copy_sem.at[i])
        for i, (source, target) in enumerate(
            (
                (packed_hbm, packed_ref),
                (target_hbm, target_table),
                (source_hbm, source_table),
                (analysis_hbm, analysis_ref),
            )
        )
    ]
    for load in loads:
        load.start()
    loads[0].wait()
    for code in range(27):
        flat_ref[code : code + 1, :] = packed_ref[code, 32:33, :].astype(jnp.int32)
    names_copy = pltpu.make_async_copy(flat_ref, names_ref, copy_sem.at[4])
    names_copy.start()
    lanes = lax.broadcasted_iota(jnp.int32, (27, 8, HEAD), 2)
    rows8 = lax.broadcasted_iota(jnp.int32, (27, 8, HEAD), 1)
    tails = packed_ref[:, 24:32, :]
    for group in range(3):
        head = packed_ref[:, 8 * group : 8 * group + 8, :]
        centre[:, 8 * group : 8 * group + 8, :] = jnp.broadcast_to(
            head[:, :, 0:1] * (0.5 / math.sqrt(math.pi)), head.shape
        )
        head = jnp.where((lanes == 0) & (rows8 + 8 * group < 12), 0.0, head)
        head_high = head.astype(jnp.bfloat16).astype(jnp.float32)
        tail = tails if group == 0 else pltpu.roll(tails, HEAD - TAIL * group, 2)
        tail = jnp.where(lanes < TAIL, tail, 0.0)
        tail_high = tail.astype(jnp.bfloat16).astype(jnp.float32)
        tail_low = tail - tail_high
        rows = slice(8 * group, 8 * group + 8)
        coef[:, rows, 0:128] = head_high
        coef[:, rows, 128:256] = head_high
        coef[:, rows, 256:384] = head - head_high
        coef[:, rows, 384:512] = (
            tail_high + pltpu.roll(tail_high, TAIL, 2) + pltpu.roll(tail_low, 2 * TAIL, 2)
        )

    own = coef[13].astype(jnp.bfloat16)
    loads[1].wait()
    row_points = lax.dot_general(own, target_table[...], NT, preferred_element_type=jnp.float32)

    slab[...] = jnp.zeros(slab.shape, jnp.float32)
    ones = jnp.ones((1, T_PAD), jnp.float32)
    for vesicle in range(4):
        x = [row_points[4 * i + vesicle : 4 * i + vesicle + 1, :] for i in range(3)]
        for i in range(3):
            slab[0, i : i + 1, 0:T_PAD] = x[i]
        slab[0, 3:4, 0:T_PAD] = ones
        slab[0, 4:5, 0:T_PAD] = x[0] * x[0] + x[1] * x[1] + x[2] * x[2] + delta2
        first, second, third = split_three(slab[0, :, 0:T_PAD])
        lifted[vesicle] = jnp.transpose(
            jnp.concatenate(
                [first, first, second, second, first, third]
                + [jnp.zeros((HEAD - 48, T_PAD), jnp.float32)]
            )
        ).astype(jnp.bfloat16)
    for copy in range(UNROLL):
        slab[copy, 4:5, :] = jnp.ones((1, S_PAD), jnp.float32)

    loads[2].wait()
    everything = coef[...].reshape(27 * 24, 512).astype(jnp.bfloat16)

    @pl.loop(0, S_PAD // CHUNK)
    def _(step):
        span = pl.ds(pl.multiple_of(step * CHUNK, CHUNK), CHUNK)
        grids[:, span] = jnp.dot(
            everything, source_table[:, span], preferred_element_type=jnp.float32
        )

    names_copy.wait()
    def scan_device(code, filled):
        def scan_slot(slot, filled):
            first = names_ref[code, slot]
            second = names_ref[code, 12 + slot]
            target_list[filled] = second & 3
            source_list[filled] = code * 4 + (first & 3)
            return filled + ((second >> 2) == 26 - code).astype(jnp.int32)

        return lax.fori_loop(0, names_ref[code, 24], scan_slot, filled)

    def own_slot(slot, filled):
        target_list[filled] = names_ref[13, slot] & 3
        source_list[filled] = names_ref[13, 12 + slot]
        return filled + 1

    filled = lax.fori_loop(0, 27, scan_device, 0)
    filled = lax.fori_loop(0, names_ref[13, 24], own_slot, filled)

    loads[3].wait()
    weight = jnp.concatenate(
        [analysis_ref[T_PAD + i : T_PAD + i + 1, :] for i in range(S_PAD // 256)], axis=1
    )
    totals[...] = jnp.zeros(totals.shape, jnp.float32)

    def process(item, columns, slab):
        target = target_list[item]
        entry = source_list[item]
        device = entry >> 2
        vesicle = entry & 3
        base = device * 24 + vesicle
        points, forces = [], []
        for i in range(3):
            moved = centre[device, pl.ds(4 * i + vesicle, 1), :] - centre[13, pl.ds(4 * i + target, 1), :]
            points.append(grids[pl.ds(base + 4 * i, 1), :] + jnp.concatenate([moved] * (S_PAD // HEAD), axis=1))
            forces.append(grids[pl.ds(base + 12 + 4 * i, 1), :] * weight)
        square = points[0] * points[0] + points[1] * points[1] + points[2] * points[2]
        for i in range(3):
            slab[i : i + 1, :] = -2.0 * points[i]
        slab[3:4, :] = square
        first, second, third = split_three(slab[...])
        right = jnp.concatenate([first, second, first, second, third, first]).astype(jnp.bfloat16)
        left = lifted[target, 0:T_ROWS, 0:48]
        square = square + 2.0 * delta2
        along = points[0] * forces[0] + points[1] * forces[1] + points[2] * forces[2]
        for i in range(3):
            columns[i : i + 1, :] = forces[i]
            for j in range(3):
                columns[3 + 3 * i + j : 4 + 3 * i + j, :] = forces[i] * points[j]
            columns[12 + i : 13 + i, :] = square * forces[i] + along * points[i]
        wide = columns[...]
        wide_high = wide.astype(jnp.bfloat16)
        wide_low = (wide - wide_high.astype(jnp.float32)).astype(jnp.bfloat16)
        both = jnp.concatenate([wide_high, wide_low], axis=0)
        parts, wides = [], []
        for step in range(S_PAD // CHUNK):
            span = slice(step * CHUNK, (step + 1) * CHUNK)
            softened = jnp.dot(left, right[:, span], preferred_element_type=jnp.float32)
            inverse = lax.rsqrt(softened)
            cube = inverse * inverse * inverse
            cube_high = cube.astype(jnp.bfloat16)
            cube_low = (cube - cube_high.astype(jnp.float32)).astype(jnp.bfloat16)
            parts += [cube_high, cube_low]
            wides += [both[:, span], both[:, span]]
        part = jnp.concatenate(parts, axis=1)
        wide = jnp.concatenate(wides, axis=1)
        total = lax.dot_general(part, wide, NT, preferred_element_type=jnp.float32)
        totals[target, 0:T_ROWS, 0 : 2 * COLS] += total

    @pl.loop(0, filled // UNROLL)
    def _(item):
        for copy in range(UNROLL):
            process(UNROLL * item + copy, columns.at[copy], slab.at[copy])

    @pl.when(filled % 4 >= 2)
    def _():
        for copy in range(2):
            process(filled // 4 * 4 + copy, columns.at[copy], slab.at[copy])

    @pl.when(filled % 2 == 1)
    def _():
        process(filled - 1, columns.at[0], slab.at[0])

    for vesicle in range(4):
        turned = jnp.transpose(totals[vesicle])
        sums = turned[0:COLS] + turned[COLS : 2 * COLS]
        x = [row_points[4 * i + vesicle : 4 * i + vesicle + 1, :] for i in range(3)]
        plain = [sums[i : i + 1, :] for i in range(3)]
        cross = [[sums[3 + 3 * i + j : 4 + 3 * i + j, :] for j in range(3)] for i in range(3)]
        last = [sums[12 + i : 13 + i, :] for i in range(3)]
        square = x[0] * x[0] + x[1] * x[1] + x[2] * x[2]
        along = x[0] * plain[0] + x[1] * plain[1] + x[2] * plain[2]
        trace = cross[0][0] + cross[1][1] + cross[2][2]
        for i in range(3):
            value = square * plain[i] + x[i] * (along - trace) + last[i]
            for j in range(3):
                value = value - x[j] * (2.0 * cross[i][j] + cross[j][i])
            columns[0, 4 * i + vesicle : 4 * i + vesicle + 1, 0:T_PAD] = value * (0.125 / math.pi)
    result = jnp.dot(
        columns[0, :, 0:T_PAD],
        analysis_ref[0:T_PAD, :],
        precision=lax.Precision.HIGHEST,
        preferred_element_type=jnp.float32,
    )
    for i in range(3):
        out_ref[i] = result[4 * i : 4 * i + 4, 0 : HEAD + TAIL]


def near(packed, tables):
    vmem = pl.BlockSpec(memory_space=pltpu.VMEM)
    return pl.pallas_call(
        near_kernel,
        out_shape=jax.ShapeDtypeStruct((3, 4, HEAD + TAIL), jnp.float32),
        in_specs=[pl.BlockSpec(memory_space=pltpu.HBM)] * 4,
        out_specs=vmem,
        scratch_shapes=[
            pltpu.VMEM((27, 24, 512), jnp.float32),
            pltpu.VMEM((27 * 24, S_PAD), jnp.float32),
            pltpu.VMEM((27, 24, HEAD), jnp.float32),
            pltpu.VMEM((4, T_PAD, HEAD), jnp.bfloat16),
            pltpu.VMEM((UNROLL, 8, S_PAD), jnp.float32),
            pltpu.VMEM((4, T_PAD, HEAD), jnp.float32),
            pltpu.VMEM((UNROLL, COLS, S_PAD), jnp.float32),
            pltpu.SMEM((360,), jnp.int32),
            pltpu.SMEM((360,), jnp.int32),
            pltpu.VMEM((27, MESSAGE, HEAD), jnp.float32),
            pltpu.VMEM((512, S_PAD), jnp.bfloat16),
            pltpu.VMEM((T_PAD, 512), jnp.bfloat16),
            pltpu.VMEM((T_PAD + 8, 256), jnp.float32),
            pltpu.VMEM((32, HEAD), jnp.int32),
            pltpu.SMEM((32, HEAD), jnp.int32),
            pltpu.SemaphoreType.DMA((5,)),
        ],
        compiler_params=pltpu.CompilerParams(vmem_limit_bytes=64 * 1024 * 1024),
        name="near",
    )(packed, *tables)


def on_device(sizes, shape_coef, density_coef, pair_count, pair_slots):
    shape, density = (
        jnp.swapaxes(part[0, 0, 0], 0, 1) for part in (shape_coef, density_coef)
    )
    slots = pair_slots[0, 0, 0].T
    packed = halo(shape, density, slots, pair_count.reshape(1, 1), sizes)
    result = near(packed, grid_tables())
    return jnp.swapaxes(result, 0, 1)[None, None, None]


def solution(mesh):
    placed = (
        P("gx", "gy", "gz", None, None, None),
        P("gx", "gy", "gz", None, None, None),
        P("gx", "gy", "gz"),
        P("gx", "gy", "gz", None, None),
    )
    return jax.shard_map(
        functools.partial(on_device, tuple(mesh.shape[axis] for axis in AXES)),
        mesh=mesh,
        in_specs=placed,
        out_specs=P("gx", "gy", "gz", None, None, None),
        check_vma=False,
    )
```

```python
import functools
import itertools
import math

import jax
import jax.numpy as jnp
import numpy as np
from jax import lax
from jax.experimental import pallas as pl
from jax.experimental.pallas import tpu as pltpu
from jax.sharding import PartitionSpec as P

P_SIZE = 12
Q = 24


blob_radius = 0.25

def gauss_nodes(node_count):
    numbers = np.arange(1, node_count + 1)
    cosine = np.cos(np.pi * (numbers - 0.25) / (node_count + 0.5))

    def legendre_pair(points):
        legendre_prev = np.ones(points.shape)
        legendre_next = np.array(points)
        for degree in range(2, node_count + 1):
            legendre_prev, legendre_next = (
                legendre_next,
                ((2.0 * degree - 1.0) * points * legendre_next - (degree - 1.0) * legendre_prev)
                / degree,
            )
        slope = node_count * (points * legendre_next - legendre_prev) / (points * points - 1.0)
        return (legendre_next, slope)

    for newton_step in range(100):
        value_now, slope = legendre_pair(cosine)
        cosine = cosine - value_now / slope
    value_now, slope = legendre_pair(cosine)
    weights = 2.0 / ((1.0 - cosine * cosine) * slope * slope)
    return (np.array(cosine[::-1]), np.array(weights[::-1]))


def harmonic_table(top_degree, latitudes, longitudes):
    cosine, gauss_weight = gauss_nodes(latitudes)
    sine_theta = np.sqrt(1.0 - cosine * cosine)
    angles = 2.0 * np.pi * np.arange(longitudes) / longitudes
    legendre = np.zeros((top_degree + 1, top_degree + 1, latitudes))
    legendre[0, 0] = np.sqrt(0.25 / np.pi)
    for degree_m in range(1, top_degree + 1):
        legendre[degree_m, degree_m] = (
            np.sqrt((2.0 * degree_m + 1.0) / (2.0 * degree_m))
            * sine_theta
            * legendre[degree_m - 1, degree_m - 1]
        )
    for degree_m in range(top_degree + 1):
        if degree_m + 1 <= top_degree:
            legendre[degree_m + 1, degree_m] = (
                np.sqrt(2.0 * degree_m + 3.0) * cosine * legendre[degree_m, degree_m]
            )
        for degree_l in range(degree_m + 2, top_degree + 1):
            factor = np.sqrt(
                (4.0 * degree_l * degree_l - 1.0) / (degree_l * degree_l - degree_m * degree_m)
            )
            lagged = np.sqrt(
                ((degree_l - 1.0) * (degree_l - 1.0) - degree_m * degree_m)
                / (4.0 * (degree_l - 1.0) * (degree_l - 1.0) - 1.0)
            )
            legendre[degree_l, degree_m] = factor * (
                cosine * legendre[degree_l - 1, degree_m]
                - lagged * legendre[degree_l - 2, degree_m]
            )
    table_rows = []
    for degree_l in range(top_degree + 1):
        for signed in range(-degree_l, degree_l + 1):
            polar_part = legendre[degree_l, abs(signed)][:, None]
            if signed > 0:
                azimuth = np.sqrt(2.0) * np.cos(signed * angles)
            elif signed < 0:
                azimuth = np.sqrt(2.0) * np.sin(-signed * angles)
            else:
                azimuth = np.ones(longitudes)
            table_rows.append((polar_part * azimuth[None, :]).reshape(-1))
    synthesis = np.stack(table_rows)
    weights = np.repeat(gauss_weight, longitudes) * (2.0 * np.pi / longitudes)
    return (synthesis, weights)

AXES = ("gx", "gy", "gz")
OFFSETS = list(itertools.product((-1, 0, 1), repeat=3))
HEAD = 128
TAIL = 41
MESSAGE = 40
T_PAD = 384
T_ROWS = 352
S_PAD = 1280
CHUNK = 1280
UNROLL = 4
COLS = 16


def split_table(table):
    high = table.astype(np.float32).astype(jnp.bfloat16)
    low = (table - high.astype(np.float64)).astype(jnp.bfloat16)
    pad = np.zeros((512 - 3 * table.shape[0], table.shape[1]), jnp.bfloat16)
    return np.concatenate(
        [high[:HEAD], low[:HEAD], high[:HEAD], high[HEAD:], low[HEAD:], high[HEAD:], pad]
    )


def grid_tables():
    target_synth, target_weight = harmonic_table(P_SIZE, P_SIZE + 1, 2 * (P_SIZE + 1))
    upsample_synth, upsample_weight = harmonic_table(P_SIZE, Q + 1, 2 * (Q + 1))
    targets, sources = target_synth.shape[1], upsample_synth.shape[1]
    target_wide = np.pad(target_synth, ((0, 0), (0, T_PAD - targets)))
    source_wide = np.pad(upsample_synth, ((0, 0), (0, S_PAD - sources)))
    weight_rows = np.pad(upsample_weight, (0, S_PAD - sources)).reshape(-1, 256)
    weight_rows = np.pad(weight_rows, ((0, 8 - weight_rows.shape[0]), (0, 0)))
    analysis = np.pad(
        (target_synth * target_weight[None, :]).T,
        ((0, T_PAD - targets), (0, 256 - target_synth.shape[0])),
    )
    return (
        jnp.asarray(split_table(source_wide)),
        jnp.asarray(np.ascontiguousarray(split_table(target_wide).T)),
        jnp.asarray(np.concatenate([analysis, weight_rows]), dtype=jnp.float32),
    )


def halo_kernel(
    sizes, shape_hbm, density_hbm, slots_hbm, count_hbm, out_ref,
    own_ref, tail_ref, blank_ref, shape_ref, density_ref, slots_ref, count_ref,
    send_sem, recv_sem, local_sem,
):
    loads = [
        pltpu.make_async_copy(source, target, local_sem.at[27 + i])
        for i, (source, target) in enumerate(
            (
                (shape_hbm, shape_ref),
                (density_hbm, density_ref),
                (slots_hbm, slots_ref),
                (count_hbm, count_ref),
            )
        )
    ]
    for load in loads:
        load.start()
    here = [lax.axis_index(axis) for axis in AXES]

    def place(offset):
        there = [h + o for h, o in zip(here, offset)]
        exists = None
        for spot, o, size in zip(there, offset, sizes):
            if o:
                inside = (spot >= 0) & (spot < size)
                exists = inside if exists is None else exists & inside
        return tuple(there), exists

    barrier = pltpu.get_barrier_semaphore()
    around = 1
    for h, size in zip(here, sizes):
        around = around * (1 + (h > 0).astype(jnp.int32) + (h < size - 1).astype(jnp.int32))
    for offset in OFFSETS:
        if any(offset):
            there, exists = place(offset)

            @pl.when(exists)
            def _():
                pl.semaphore_signal(
                    barrier, inc=1, device_id=there, device_id_type=pl.DeviceIdType.MESH
                )

    blank_ref[...] = jnp.zeros(blank_ref.shape, jnp.float32)
    tail_ref[...] = jnp.zeros(tail_ref.shape, jnp.float32)
    for load in loads:
        load.wait()
    for start, source in ((0, shape_ref), (12, density_ref)):
        for i in range(3):
            rows = slice(start + 4 * i, start + 4 * i + 4)
            own_ref[rows, :] = source[i, :, 0:HEAD]
            tail_ref[rows, 0:TAIL] = source[i, :, HEAD : HEAD + TAIL]
    own_ref[24:32, :] = (
        tail_ref[0:8, :]
        + pltpu.roll(tail_ref[8:16, :], TAIL, 1)
        + pltpu.roll(tail_ref[16:24, :], 2 * TAIL, 1)
    )
    names = jnp.full((1, HEAD), count_ref[0, 0].astype(jnp.float32))
    own_ref[32:MESSAGE, :] = jnp.broadcast_to(names, (MESSAGE - 32, HEAD))
    for i in range(2):
        own_ref[32:33, 12 * i : 12 * i + 12] = slots_ref[i : i + 1, :].astype(jnp.float32)
    pl.semaphore_wait(barrier, around - 1)

    def transfer(code):
        there, exists = place(OFFSETS[code])
        copy = pltpu.make_async_remote_copy(
            src_ref=own_ref,
            dst_ref=out_ref.at[26 - code],
            send_sem=send_sem.at[code],
            recv_sem=recv_sem.at[26 - code],
            device_id=there,
            device_id_type=pl.DeviceIdType.MESH,
        )
        return copy, exists

    farthest = sorted(range(27), key=lambda code: -sum(abs(o) for o in OFFSETS[code]))
    for code in farthest:
        if code != 13:
            copy, exists = transfer(code)

            @pl.when(exists)
            def _():
                copy.start()

    def fill(code):
        source = own_ref if code == 13 else blank_ref
        return pltpu.make_async_copy(source, out_ref.at[code], local_sem.at[code])

    fill(13).start()
    for code in range(27):
        if code != 13:
            there, exists = place(OFFSETS[code])

            @pl.when(jnp.logical_not(exists))
            def _():
                fill(code).start()

    fill(13).wait()
    for code in range(27):
        if code != 13:
            there, exists = place(OFFSETS[code])

            @pl.when(jnp.logical_not(exists))
            def _():
                fill(code).wait()

    for code in range(27):
        if code != 13:
            there, exists = place(OFFSETS[code])

            @pl.when(exists)
            def _():
                copy = pltpu.make_async_remote_copy(
                    src_ref=own_ref,
                    dst_ref=out_ref.at[code],
                    send_sem=send_sem.at[code],
                    recv_sem=recv_sem.at[code],
                    device_id=there,
                    device_id_type=pl.DeviceIdType.MESH,
                )
                copy.wait()


def halo(shape, density, slots, count, sizes):
    hbm = pl.BlockSpec(memory_space=pltpu.HBM)
    return pl.pallas_call(
        functools.partial(halo_kernel, sizes),
        out_shape=jax.ShapeDtypeStruct((27, MESSAGE, HEAD), jnp.float32),
        in_specs=[hbm] * 4,
        out_specs=hbm,
        scratch_shapes=[
            pltpu.VMEM((MESSAGE, HEAD), jnp.float32),
            pltpu.VMEM((24, HEAD), jnp.float32),
            pltpu.VMEM((MESSAGE, HEAD), jnp.float32),
            pltpu.VMEM(shape.shape, jnp.float32),
            pltpu.VMEM(density.shape, jnp.float32),
            pltpu.VMEM(slots.shape, jnp.int32),
            pltpu.SMEM(count.shape, jnp.int32),
            pltpu.SemaphoreType.DMA((27,)),
            pltpu.SemaphoreType.DMA((27,)),
            pltpu.SemaphoreType.DMA((31,)),
        ],
        compiler_params=pltpu.CompilerParams(collective_id=0, has_side_effects=True),
        name="halo",
    )(shape, density, slots, count)


NT = (((1,), (1,)), ((), ()))


def split_three(value):
    first = value.astype(jnp.bfloat16).astype(jnp.float32)
    rest = value - first
    second = rest.astype(jnp.bfloat16).astype(jnp.float32)
    return first, second, rest - second


def near_kernel(
    packed_hbm, source_hbm, target_hbm, analysis_hbm, out_ref,
    coef, grids, centre, lifted, slab, totals, columns, target_list, source_list,
    packed_ref, source_table, target_table, analysis_ref, flat_ref, names_ref, copy_sem,
):
    delta2 = blob_radius * blob_radius
    loads = [
        pltpu.make_async_copy(source, target, copy_sem.at[i])
        for i, (source, target) in enumerate(
            (
                (packed_hbm, packed_ref),
                (target_hbm, target_table),
                (source_hbm, source_table),
                (analysis_hbm, analysis_ref),
            )
        )
    ]
    for load in loads:
        load.start()
    loads[0].wait()
    for code in range(27):
        flat_ref[code : code + 1, :] = packed_ref[code, 32:33, :].astype(jnp.int32)
    names_copy = pltpu.make_async_copy(flat_ref, names_ref, copy_sem.at[4])
    names_copy.start()
    lanes = lax.broadcasted_iota(jnp.int32, (27, 8, HEAD), 2)
    rows8 = lax.broadcasted_iota(jnp.int32, (27, 8, HEAD), 1)
    tails = packed_ref[:, 24:32, :]
    for group in range(3):
        head = packed_ref[:, 8 * group : 8 * group + 8, :]
        centre[:, 8 * group : 8 * group + 8, :] = jnp.broadcast_to(
            head[:, :, 0:1] * (0.5 / math.sqrt(math.pi)), head.shape
        )
        head = jnp.where((lanes == 0) & (rows8 + 8 * group < 12), 0.0, head)
        head_high = head.astype(jnp.bfloat16).astype(jnp.float32)
        tail = tails if group == 0 else pltpu.roll(tails, HEAD - TAIL * group, 2)
        tail = jnp.where(lanes < TAIL, tail, 0.0)
        tail_high = tail.astype(jnp.bfloat16).astype(jnp.float32)
        tail_low = tail - tail_high
        rows = slice(8 * group, 8 * group + 8)
        coef[:, rows, 0:128] = head_high
        coef[:, rows, 128:256] = head_high
        coef[:, rows, 256:384] = head - head_high
        coef[:, rows, 384:512] = (
            tail_high + pltpu.roll(tail_high, TAIL, 2) + pltpu.roll(tail_low, 2 * TAIL, 2)
        )

    own = coef[13].astype(jnp.bfloat16)
    loads[1].wait()
    row_points = lax.dot_general(own, target_table[...], NT, preferred_element_type=jnp.float32)

    slab[...] = jnp.zeros(slab.shape, jnp.float32)
    ones = jnp.ones((1, T_PAD), jnp.float32)
    for vesicle in range(4):
        x = [row_points[4 * i + vesicle : 4 * i + vesicle + 1, :] for i in range(3)]
        for i in range(3):
            slab[0, i : i + 1, 0:T_PAD] = x[i]
        slab[0, 3:4, 0:T_PAD] = ones
        slab[0, 4:5, 0:T_PAD] = x[0] * x[0] + x[1] * x[1] + x[2] * x[2] + delta2
        first, second, third = split_three(slab[0, :, 0:T_PAD])
        lifted[vesicle] = jnp.transpose(
            jnp.concatenate(
                [first, first, second, second, first, third]
                + [jnp.zeros((HEAD - 48, T_PAD), jnp.float32)]
            )
        ).astype(jnp.bfloat16)
    for copy in range(UNROLL):
        slab[copy, 4:5, :] = jnp.ones((1, S_PAD), jnp.float32)

    loads[2].wait()
    everything = coef[...].reshape(27 * 24, 512).astype(jnp.bfloat16)

    @pl.loop(0, S_PAD // CHUNK)
    def _(step):
        span = pl.ds(pl.multiple_of(step * CHUNK, CHUNK), CHUNK)
        grids[:, span] = jnp.dot(
            everything, source_table[:, span], preferred_element_type=jnp.float32
        )

    names_copy.wait()
    def scan_device(code, filled):
        def scan_slot(slot, filled):
            first = names_ref[code, slot]
            second = names_ref[code, 12 + slot]
            target_list[filled] = second & 3
            source_list[filled] = code * 4 + (first & 3)
            return filled + ((second >> 2) == 26 - code).astype(jnp.int32)

        return lax.fori_loop(0, names_ref[code, 24], scan_slot, filled)

    def own_slot(slot, filled):
        target_list[filled] = names_ref[13, slot] & 3
        source_list[filled] = names_ref[13, 12 + slot]
        return filled + 1

    filled = lax.fori_loop(0, 27, scan_device, 0)
    filled = lax.fori_loop(0, names_ref[13, 24], own_slot, filled)

    loads[3].wait()
    weight = jnp.concatenate(
        [analysis_ref[T_PAD + i : T_PAD + i + 1, :] for i in range(S_PAD // 256)], axis=1
    )
    totals[...] = jnp.zeros(totals.shape, jnp.float32)

    def process(item, columns, slab):
        target = target_list[item]
        entry = source_list[item]
        device = entry >> 2
        vesicle = entry & 3
        base = device * 24 + vesicle
        points, forces = [], []
        for i in range(3):
            moved = centre[device, pl.ds(4 * i + vesicle, 1), :] - centre[13, pl.ds(4 * i + target, 1), :]
            points.append(grids[pl.ds(base + 4 * i, 1), :] + jnp.concatenate([moved] * (S_PAD // HEAD), axis=1))
            forces.append(grids[pl.ds(base + 12 + 4 * i, 1), :] * weight)
        square = points[0] * points[0] + points[1] * points[1] + points[2] * points[2]
        for i in range(3):
            slab[i : i + 1, :] = -2.0 * points[i]
        slab[3:4, :] = square
        first, second, third = split_three(slab[...])
        right = jnp.concatenate([first, second, first, second, third, first]).astype(jnp.bfloat16)
        left = lifted[target, 0:T_ROWS, 0:48]
        square = square + 2.0 * delta2
        along = points[0] * forces[0] + points[1] * forces[1] + points[2] * forces[2]
        for i in range(3):
            columns[i : i + 1, :] = forces[i]
            for j in range(3):
                columns[3 + 3 * i + j : 4 + 3 * i + j, :] = forces[i] * points[j]
            columns[12 + i : 13 + i, :] = square * forces[i] + along * points[i]
        wide = columns[...]
        wide_high = wide.astype(jnp.bfloat16)
        wide_low = (wide - wide_high.astype(jnp.float32)).astype(jnp.bfloat16)
        both = jnp.concatenate([wide_high, wide_low], axis=0)
        parts, wides = [], []
        for step in range(S_PAD // CHUNK):
            span = slice(step * CHUNK, (step + 1) * CHUNK)
            softened = jnp.dot(left, right[:, span], preferred_element_type=jnp.float32)
            inverse = lax.rsqrt(softened)
            cube = inverse * inverse * inverse
            cube_high = cube.astype(jnp.bfloat16)
            cube_low = (cube - cube_high.astype(jnp.float32)).astype(jnp.bfloat16)
            parts += [cube_high, cube_low]
            wides += [both[:, span], both[:, span]]
        part = jnp.concatenate(parts, axis=1)
        wide = jnp.concatenate(wides, axis=1)
        total = lax.dot_general(part, wide, NT, preferred_element_type=jnp.float32)
        totals[target, 0:T_ROWS, 0 : 2 * COLS] += total

    @pl.loop(0, filled // UNROLL)
    def _(item):
        for copy in range(UNROLL):
            process(UNROLL * item + copy, columns.at[copy], slab.at[copy])

    @pl.when(filled % 4 >= 2)
    def _():
        for copy in range(2):
            process(filled // 4 * 4 + copy, columns.at[copy], slab.at[copy])

    @pl.when(filled % 2 == 1)
    def _():
        process(filled - 1, columns.at[0], slab.at[0])

    for vesicle in range(4):
        turned = jnp.transpose(totals[vesicle])
        sums = turned[0:COLS] + turned[COLS : 2 * COLS]
        x = [row_points[4 * i + vesicle : 4 * i + vesicle + 1, :] for i in range(3)]
        plain = [sums[i : i + 1, :] for i in range(3)]
        cross = [[sums[3 + 3 * i + j : 4 + 3 * i + j, :] for j in range(3)] for i in range(3)]
        last = [sums[12 + i : 13 + i, :] for i in range(3)]
        square = x[0] * x[0] + x[1] * x[1] + x[2] * x[2]
        along = x[0] * plain[0] + x[1] * plain[1] + x[2] * plain[2]
        trace = cross[0][0] + cross[1][1] + cross[2][2]
        for i in range(3):
            value = square * plain[i] + x[i] * (along - trace) + last[i]
            for j in range(3):
                value = value - x[j] * (2.0 * cross[i][j] + cross[j][i])
            columns[0, 4 * i + vesicle : 4 * i + vesicle + 1, 0:T_PAD] = value * (0.125 / math.pi)
    result = jnp.dot(
        columns[0, :, 0:T_PAD],
        analysis_ref[0:T_PAD, :],
        precision=lax.Precision.HIGHEST,
        preferred_element_type=jnp.float32,
    )
    for i in range(3):
        out_ref[i] = result[4 * i : 4 * i + 4, 0 : HEAD + TAIL]


def near(packed, tables):
    vmem = pl.BlockSpec(memory_space=pltpu.VMEM)
    return pl.pallas_call(
        near_kernel,
        out_shape=jax.ShapeDtypeStruct((3, 4, HEAD + TAIL), jnp.float32),
        in_specs=[pl.BlockSpec(memory_space=pltpu.HBM)] * 4,
        out_specs=vmem,
        scratch_shapes=[
            pltpu.VMEM((27, 24, 512), jnp.float32),
            pltpu.VMEM((27 * 24, S_PAD), jnp.float32),
            pltpu.VMEM((27, 24, HEAD), jnp.float32),
            pltpu.VMEM((4, T_PAD, HEAD), jnp.bfloat16),
            pltpu.VMEM((UNROLL, 8, S_PAD), jnp.float32),
            pltpu.VMEM((4, T_PAD, HEAD), jnp.float32),
            pltpu.VMEM((UNROLL, COLS, S_PAD), jnp.float32),
            pltpu.SMEM((360,), jnp.int32),
            pltpu.SMEM((360,), jnp.int32),
            pltpu.VMEM((27, MESSAGE, HEAD), jnp.float32),
            pltpu.VMEM((512, S_PAD), jnp.bfloat16),
            pltpu.VMEM((T_PAD, 512), jnp.bfloat16),
            pltpu.VMEM((T_PAD + 8, 256), jnp.float32),
            pltpu.VMEM((32, HEAD), jnp.int32),
            pltpu.SMEM((32, HEAD), jnp.int32),
            pltpu.SemaphoreType.DMA((5,)),
        ],
        compiler_params=pltpu.CompilerParams(vmem_limit_bytes=64 * 1024 * 1024),
        name="near",
    )(packed, *tables)


def on_device(sizes, shape_coef, density_coef, pair_count, pair_slots):
    shape, density = (
        jnp.swapaxes(part[0, 0, 0], 0, 1) for part in (shape_coef, density_coef)
    )
    slots = pair_slots[0, 0, 0].T
    packed = halo(shape, density, slots, pair_count.reshape(1, 1), sizes)
    result = near(packed, grid_tables())
    return jnp.swapaxes(result, 0, 1)[None, None, None]


def solution(mesh):
    placed = (
        P("gx", "gy", "gz", None, None, None),
        P("gx", "gy", "gz", None, None, None),
        P("gx", "gy", "gz"),
        P("gx", "gy", "gz", None, None),
    )
    return jax.shard_map(
        functools.partial(on_device, tuple(mesh.shape[axis] for axis in AXES)),
        mesh=mesh,
        in_specs=placed,
        out_specs=P("gx", "gy", "gz", None, None, None),
        check_vma=False,
    )
```
